256 devices in a mesh: seq: 32 (over z, y), pb: 8 (over x, core).
Axes of the slice: x: 4, y: 4, z: 8, core: 2. Of those that a mesh axis runs over, the one named last changes fastest.
Arguments:
- queries: bfloat16 [8, 4096, 4096], P('pb', 'seq'), may hold values from -6 to 6
- keys: bfloat16 [8, 4096, 1024], P('pb', 'seq'), may hold values from -6 to 6
- values: bfloat16 [8, 4096, 1024], P('pb', 'seq'), may hold values from -18 to 18
- query_gain: float32 [128], replicated, may hold values from 0.1 to 1.9
- key_gain: float32 [128], replicated, may hold values from 0.1 to 1.9
- doc_lengths: int32 [8, 16], P('pb'), may hold values from 1 to 512, 4096 in all within a row
- span_lengths: int32 [8, 128], P('pb'), may hold values from 1 to 64, 4096 in all within a row
- query_emb: bfloat16 [512, 4096], P('pb', 'seq'), may hold values from -0.09375 to 0.09375
- answer_options: int32 [512, 8], replicated, may hold values from 0 to 1023, all different within a row
Outputs:
- query_loss: float32 [512], P('pb')
- query_grad: bfloat16 [8, 4096, 4096], P('pb', 'seq')
- key_grad: bfloat16 [8, 4096, 1024], P('pb', 'seq')
- value_grad: bfloat16 [8, 4096, 1024], P('pb', 'seq')
The draws below stay inside these ranges and needn't reach their ends.
Inputs may be any that keep to these rules, and one draw needn't show every extreme that they name: `doc_lengths`: row p is the documents of sequence p in order; they sum to 4096, and the longest has exactly 512 tokens. `span_lengths`: row p is the spans of sequence p in order; they sum to 4096, and the longest has exactly 64 tokens. `answer_options`: span p * 128 + c is span c of sequence p. The 8 entries of a row differ; column 0 is the positive. Every span is named by some row.
All inputs are finite; a program needn't handle non-finite values.
Results may differ from the reference program's by a relative error of at most 0.02.
Values may be sent and summed in bfloat16 or wider, within the bound.
A program may use at most 64 MiB of HBM per device.

```python
import math
import jax
import jax.numpy as jnp
import numpy as np
from jax import lax

QUERY_HEADS = 32
KEY_VALUE_HEADS = 8
HEAD_SIZE = 128
D = 4096
SEQUENCE_TOKENS = 4096
DOC_MAX = 512
NDOC = 16
CH_MAX = 64
NCH = 128
NQ_ALL = 512
CAND = 8
N_PB = 8


def draw_values(key, part):
    key = jax.random.fold_in(key, 7)
    head_random_key, jitter_random_key = jax.random.split(key, 2)
    head_position = jnp.arange(KEY_VALUE_HEADS, dtype=jnp.float32).reshape(1, 1, KEY_VALUE_HEADS, 1) / (KEY_VALUE_HEADS - 1)
    head_multiplier = 3.0 ** head_position * jnp.exp(jax.random.uniform(head_random_key, (N_PB, 1, KEY_VALUE_HEADS, 1), minval=-0.35, maxval=0.35))
    random_jitter = jnp.clip(jax.random.normal(jitter_random_key, (N_PB, SEQUENCE_TOKENS, KEY_VALUE_HEADS, HEAD_SIZE)), -4.0, 4.0)
    return (random_jitter * head_multiplier).reshape(N_PB, SEQUENCE_TOKENS, KEY_VALUE_HEADS * HEAD_SIZE).astype(jnp.bfloat16)


def level_of(own_key, dims, pieces, least, top_value):
    def one(dim, blocks):
        steps = jax.random.uniform(jax.random.fold_in(jax.random.fold_in(own_key, 6), dim), (blocks,), jnp.float32, least / len(pieces), top_value / len(pieces))
        return jnp.repeat(jnp.exp(steps), dims[dim] // blocks).reshape((-1,) + (1,) * (len(dims) - dim - 1))

    factor_of = one(*pieces[0])
    for cut in pieces[1:]:
        factor_of = factor_of * one(*cut)
    return factor_of


def distinct(own_key, rows, amount, top, lift):
    sequence = jax.random.permutation(jax.random.fold_in(own_key, 1), amount)
    boost = sequence
    for power in range(3):
        boost = boost * boost // amount
    boost = boost * lift // amount
    tickets = jax.random.randint(jax.random.fold_in(own_key, 2), (rows, amount), 0, 4096) + boost
    holders = jax.random.permutation(jax.random.fold_in(own_key, 3), rows)[jnp.arange(amount) % rows]
    tickets = jnp.where(jnp.arange(rows)[:, None] == holders[None, :], 1 << 14, tickets)
    merit = tickets * amount + jnp.arange(amount)
    return lax.top_k(merit.astype(jnp.int32), top)[1].astype(jnp.int32)


def split_up(count, total, most, skew):
    weights = [(1 << 20) // math.isqrt(standing ** skew) + 1 for standing in range(2, count + 1)]
    surplus, holding = total - most - (count - 1), [1] * (count - 1)
    while surplus > 0:
        candidates = [i for i in range(count - 1) if holding[i] < most]
        mass, remaining = sum([weights[i] for i in candidates]), surplus
        for i in candidates:
            addition = min(most - holding[i], max(1, remaining * weights[i] // mass), surplus)
            holding[i] = holding[i] + addition
            surplus = surplus - addition
    return np.array([most] + holding)


def ragged(rng, count, total, bound, skew):
    if count == 2:
        one = jax.random.randint(rng, (), max(1, total - bound), min(bound, total - 1) + 1)
        return jnp.stack([one, total - one])
    tallies = jnp.asarray(split_up(count, total, bound, skew), jnp.int32)
    pairs = (count - 1) // 2
    giver, receiver = tallies[1:1 + 2 * pairs:2], tallies[2:2 + 2 * pairs:2]
    slack = jnp.minimum(giver - 1, bound - receiver)
    shifted = jax.random.randint(jax.random.fold_in(rng, 1), (pairs,), 0, 1 << 20) % (slack + 1)
    tallies = tallies.at[1:1 + 2 * pairs:2].set(giver - shifted).at[2:2 + 2 * pairs:2].set(receiver + shifted)
    return tallies[jax.random.permutation(jax.random.fold_in(rng, 2), count)]


def gaussian(own_key, shape, deviation, most, cuts=(), held_as=jnp.bfloat16):
    values = deviation * jax.random.normal(own_key, shape, jnp.float32)
    if cuts:
        values = values * level_of(own_key, shape, cuts, -0.22, 0.18)
    return jnp.clip(values, -most, most).astype(held_as)


def setup_inputs(seed: int = 0) -> dict:
    arg_keys = jax.random.split(jax.random.key(seed), 10)
    queries = gaussian(arg_keys[0], (N_PB, SEQUENCE_TOKENS, QUERY_HEADS * HEAD_SIZE), 1.0, 6.0, ((0, 8), (1, 32)))
    keys = gaussian(arg_keys[1], (N_PB, SEQUENCE_TOKENS, KEY_VALUE_HEADS * HEAD_SIZE), 1.0, 6.0, ((0, 8), (1, 32)))
    values = draw_values(jax.random.fold_in(arg_keys[9], 71), 0)
    query_gain = jnp.clip(1.0 + 0.18 * jax.random.normal(arg_keys[3], (HEAD_SIZE,), jnp.float32), 0.1, 1.9)
    key_gain = jnp.clip(1.0 + 0.18 * jax.random.normal(arg_keys[4], (HEAD_SIZE,), jnp.float32), 0.1, 1.9)
    doc_lengths = jax.vmap(lambda own: ragged(own, NDOC, SEQUENCE_TOKENS, DOC_MAX, 2))(jax.random.split(arg_keys[5], N_PB)).reshape((N_PB, NDOC)).astype(jnp.int32)
    span_lengths = jax.vmap(lambda own: ragged(own, NCH, SEQUENCE_TOKENS, CH_MAX, 1))(jax.random.split(arg_keys[6], N_PB)).reshape((N_PB, NCH)).astype(jnp.int32)
    query_emb = gaussian(arg_keys[7], (NQ_ALL, D), D ** -0.5, 0.09375, ((0, 8), (1, 32)))
    answer_options = distinct(arg_keys[8], NQ_ALL, N_PB * NCH, CAND, 128)
    return dict(queries=queries, keys=keys, values=values, query_gain=query_gain, key_gain=key_gain, doc_lengths=doc_lengths, span_lengths=span_lengths, query_emb=query_emb, answer_options=answer_options)


norm_epsilon = 1e-06
softmax_divisor = 0.05
backprop_factor = 256.0

def segment_index(lengths_row, length):
    lengths_row = lengths_row.astype(jnp.int32)
    first_rows = (jnp.cumsum(lengths_row) - lengths_row).astype(jnp.int32)
    positions = jnp.arange(length, dtype=jnp.int32)
    found = lax.optimization_barrier(jnp.sum((positions[:, None] >= first_rows[None, :]).astype(jnp.int32), axis=1))
    return ((found - 1).astype(jnp.int32), first_rows)

def block_window(row_first, first_rows, length, window):
    doc_first = jnp.max(jnp.where(first_rows <= row_first, first_rows, 0))
    return jnp.minimum(doc_first, length - window).astype(jnp.int32)

def normalize_rows(entries, gain):
    as_float = entries.astype(jnp.float32)
    recip = lax.rsqrt(lax.optimization_barrier(jnp.mean(as_float * as_float, axis=-1, keepdims=True)) + norm_epsilon)
    return (as_float * recip * gain).astype(jnp.bfloat16)

def normalize_grad(entries, gain, upstream):
    as_float = entries.astype(jnp.float32)
    recip = lax.rsqrt(lax.optimization_barrier(jnp.mean(as_float * as_float, axis=-1, keepdims=True)) + norm_epsilon)
    gained = gain * upstream
    return recip * gained - as_float * recip ** 3 * lax.optimization_barrier(jnp.mean(as_float * gained, axis=-1, keepdims=True))

def product(form, left, right):
    return jnp.einsum(form, left.astype(jnp.float32), right.astype(jnp.float32), precision=lax.Precision.HIGHEST)

def attend_forward(normalized_query, normalized_key, single_value_head, doc_ids, first_rows):
    length, heads, width = normalized_query.shape
    rows = min(512, length)
    window = min(rows + 2 * DOC_MAX, length)
    score_scale = width ** (-0.5)

    def one_block(block_index):
        row_first = (block_index * rows).astype(jnp.int32)
        window_first = block_window(row_first, first_rows, length, window)
        query_block = lax.dynamic_slice_in_dim(normalized_query, row_first, rows, 0)
        key_block = lax.dynamic_slice_in_dim(normalized_key, window_first, window, 0)
        value_block = lax.dynamic_slice_in_dim(single_value_head, window_first, window, 0)
        same_doc = lax.dynamic_slice_in_dim(doc_ids, row_first, rows, 0)[:, None] == lax.dynamic_slice_in_dim(doc_ids, window_first, window, 0)[None, :]
        scores = product('qhd,kd->hqk', query_block, key_block) * score_scale
        weights = jnp.where(same_doc[None], jnp.exp(scores), 0.0)
        totals = lax.optimization_barrier(jnp.sum(weights, axis=-1))
        probs = (weights / totals[:, :, None]).astype(jnp.bfloat16)
        attended_output = product('hqk,kd->qhd', probs, value_block).astype(jnp.bfloat16)
        return (attended_output, jnp.log(totals).T)
    attended_output, logarithm_totals = lax.map(one_block, jnp.arange(length // rows, dtype=jnp.int32))
    return (attended_output.reshape(length, heads, width), logarithm_totals.reshape(length, heads))

def attend_backward(normalized_query, normalized_key, single_value_head, attended_output, logarithm_totals, attn_grad, doc_ids, first_rows):
    length, heads, width = normalized_query.shape
    rows = min(512, length)
    window = min(rows + 2 * DOC_MAX, length)
    score_scale = width ** (-0.5)
    delta = lax.optimization_barrier(jnp.sum(attn_grad.astype(jnp.float32) * attended_output.astype(jnp.float32), axis=-1))

    def one_block(carry, block_index):
        key_total, value_total = carry
        row_first = (block_index * rows).astype(jnp.int32)
        window_first = block_window(row_first, first_rows, length, window)
        query_block = lax.dynamic_slice_in_dim(normalized_query, row_first, rows, 0)
        key_block = lax.dynamic_slice_in_dim(normalized_key, window_first, window, 0)
        value_block = lax.dynamic_slice_in_dim(single_value_head, window_first, window, 0)
        grad_block = lax.dynamic_slice_in_dim(attn_grad, row_first, rows, 0)
        lse_block = lax.dynamic_slice_in_dim(logarithm_totals, row_first, rows, 0)
        delta_block = lax.dynamic_slice_in_dim(delta, row_first, rows, 0)
        same_doc = lax.dynamic_slice_in_dim(doc_ids, row_first, rows, 0)[:, None] == lax.dynamic_slice_in_dim(doc_ids, window_first, window, 0)[None, :]
        scores = product('qhd,kd->hqk', query_block, key_block) * score_scale
        recomputed = jnp.where(same_doc[None], jnp.exp(scores - lse_block.T[:, :, None]), 0.0)
        value_part = product('hqk,qhd->kd', recomputed.astype(jnp.bfloat16), grad_block)
        prob_grad = product('qhd,kd->hqk', grad_block, value_block)
        score_grad = (recomputed * (prob_grad - delta_block.T[:, :, None]) * score_scale).astype(jnp.bfloat16)
        query_part = product('hqk,kd->qhd', score_grad, key_block)
        key_part = product('hqk,qhd->kd', score_grad, query_block)
        key_total = lax.dynamic_update_slice_in_dim(key_total, lax.dynamic_slice_in_dim(key_total, window_first, window, 0) + key_part, window_first, 0)
        value_total = lax.dynamic_update_slice_in_dim(value_total, lax.dynamic_slice_in_dim(value_total, window_first, window, 0) + value_part, window_first, 0)
        return ((key_total, value_total), query_part)
    empty = jnp.zeros((length, width), jnp.float32)
    (key_total, value_total), query_parts = lax.scan(one_block, (empty, empty), jnp.arange(length // rows, dtype=jnp.int32))
    return (query_parts.reshape(length, heads, width), key_total, value_total)

def reference(queries, keys, values, query_gain, key_gain, doc_lengths, span_lengths, query_emb, answer_options):
    query_group_count = QUERY_HEADS // KEY_VALUE_HEADS
    span_blocks = []
    saved_residuals = []
    layouts = []
    for memory_bank_index in range(N_PB):
        doc_ids, first_rows = segment_index(doc_lengths[memory_bank_index], SEQUENCE_TOKENS)
        span_ids, span_firsts = segment_index(span_lengths[memory_bank_index], SEQUENCE_TOKENS)
        layouts.append((doc_ids, first_rows, span_ids))
        head_outputs = []
        for key_value_index in range(KEY_VALUE_HEADS):
            single_query_head = queries[memory_bank_index][:, key_value_index * query_group_count * HEAD_SIZE:(key_value_index + 1) * query_group_count * HEAD_SIZE].reshape(SEQUENCE_TOKENS, query_group_count, HEAD_SIZE)
            single_key_head = keys[memory_bank_index][:, key_value_index * HEAD_SIZE:(key_value_index + 1) * HEAD_SIZE]
            single_value_head = values[memory_bank_index][:, key_value_index * HEAD_SIZE:(key_value_index + 1) * HEAD_SIZE]
            normalized_query = normalize_rows(single_query_head, query_gain)
            normalized_key = normalize_rows(single_key_head, key_gain)
            attended_output, logarithm_totals = attend_forward(normalized_query, normalized_key, single_value_head, doc_ids, first_rows)
            head_outputs.append(attended_output.reshape(SEQUENCE_TOKENS, query_group_count * HEAD_SIZE))
            saved_residuals.append((single_query_head, single_key_head, single_value_head, normalized_query, normalized_key, attended_output, logarithm_totals))
        attended_all = jnp.concatenate(head_outputs, axis=1)
        span_table = (span_ids[None, :] == jnp.arange(NCH, dtype=jnp.int32)[:, None]).astype(jnp.float32)
        span_sums = jnp.dot(span_table, attended_all.astype(jnp.float32), precision=lax.Precision.HIGHEST)
        span_sizes = span_lengths[memory_bank_index].astype(jnp.float32)
        span_blocks.append((span_sums / span_sizes[:, None]).astype(jnp.bfloat16))
    span_emb = jnp.concatenate(span_blocks, axis=0)
    query_float = query_emb.astype(jnp.float32)
    whole_similarity_matrix = jnp.dot(query_float, span_emb.astype(jnp.float32).T, precision=lax.Precision.HIGHEST)
    similarity_pool = jnp.take_along_axis(whole_similarity_matrix, answer_options, axis=1) / softmax_divisor
    exponentiated_similarities = jnp.exp(similarity_pool)
    similarity_line_sums_per_query = lax.optimization_barrier(jnp.sum(exponentiated_similarities, axis=1))
    query_loss = jnp.log(similarity_line_sums_per_query) - similarity_pool[:, 0]
    correct_answer_ids = (jnp.arange(CAND, dtype=jnp.int32) == 0).astype(jnp.float32)
    ranking_objective_factor = backprop_factor * (exponentiated_similarities / similarity_line_sums_per_query[:, None] - correct_answer_ids[None, :]) / softmax_divisor
    bank_ids = jnp.arange(N_PB * NCH, dtype=jnp.int32)
    dense = lax.optimization_barrier(jnp.sum(ranking_objective_factor[:, :, None] * (answer_options[:, :, None] == bank_ids[None, None, :]).astype(jnp.float32), axis=1))
    span_grad = jnp.dot(dense.T, query_float, precision=lax.Precision.HIGHEST)
    query_grads = []
    key_grads = []
    value_grads = []
    for memory_bank_index in range(N_PB):
        doc_ids, first_rows, span_ids = layouts[memory_bank_index]
        span_sizes = span_lengths[memory_bank_index].astype(jnp.float32)
        scaled = span_grad[memory_bank_index * NCH:(memory_bank_index + 1) * NCH] / span_sizes[:, None]
        attn_grad_all = jnp.take(scaled, span_ids, axis=0).astype(jnp.bfloat16)
        query_parts = []
        key_parts = []
        value_parts = []
        for key_value_index in range(KEY_VALUE_HEADS):
            single_query_head, single_key_head, single_value_head, normalized_query, normalized_key, attended_output, logarithm_totals = saved_residuals[memory_bank_index * KEY_VALUE_HEADS + key_value_index]
            attn_grad = attn_grad_all[:, key_value_index * query_group_count * HEAD_SIZE:(key_value_index + 1) * query_group_count * HEAD_SIZE].reshape(SEQUENCE_TOKENS, query_group_count, HEAD_SIZE)
            normed_qgrad, normed_kgrad, value_total = attend_backward(normalized_query, normalized_key, single_value_head, attended_output, logarithm_totals, attn_grad, doc_ids, first_rows)
            query_parts.append(normalize_grad(single_query_head, query_gain, normed_qgrad).astype(jnp.bfloat16).reshape(SEQUENCE_TOKENS, query_group_count * HEAD_SIZE))
            key_parts.append(normalize_grad(single_key_head, key_gain, normed_kgrad).astype(jnp.bfloat16))
            value_parts.append(value_total.astype(jnp.bfloat16))
        query_grads.append(jnp.concatenate(query_parts, axis=1))
        key_grads.append(jnp.concatenate(key_parts, axis=1))
        value_grads.append(jnp.concatenate(value_parts, axis=1))
    return (query_loss, jnp.stack(query_grads), jnp.stack(key_grads), jnp.stack(value_grads))
```

```python
import functools
import math

import jax
import jax.numpy as jnp
from jax import lax
from jax.experimental import pallas as pl
from jax.experimental.pallas import tpu as pltpu
from jax.sharding import PartitionSpec as P

WIDTH = 128
NY = 4
NZ = 8
NPB = 8
BLOCK = 128
ROWS = 512
WINDOW = 1152
CHUNK = 384
SPANS = 128
QUERIES = 512
CAND = 8
EPS = 1e-06
MASKED = 16384.0
LOG2E = math.log2(math.e)
SCALE = 1.0 / math.sqrt(WIDTH)
F32 = jnp.float32
BF16 = jnp.bfloat16
MESH = pl.DeviceIdType.MESH
NT = (((1,), (1,)), ((), ()))


def dot(a, b):
    return jnp.dot(a, b, preferred_element_type=F32)


def dot_nt(a, b):
    return lax.dot_general(a, b, NT, preferred_element_type=F32)


def iota(shape, dim):
    return lax.broadcasted_iota(jnp.int32, shape, dim)


def aligned(start, size, unit=128):
    return pl.ds(pl.multiple_of(start, unit), size)


def column(row):
    return jnp.transpose(jnp.broadcast_to(row, (128, 128)))


def segments(lens):
    down = column(lens)
    across = jnp.broadcast_to(lens, (128, 128))
    sub, lane = iota((128, 128), 0), iota((128, 128), 1)
    first_row = jnp.sum(jnp.where(sub < lane, down, 0.0), axis=0, keepdims=True)
    first_col = jnp.sum(jnp.where(lane < sub, across, 0.0), axis=1, keepdims=True)
    return first_row, first_row + lens, first_col, first_col + down[:, :1]


def body(
    q_ref, k_ref, v_ref, e_ref, qgain_ref, kgain_ref, dlen_ref, slen_ref, ans_ref,
    loss_ref, gq_ref, gk_ref, gv_ref,
    qraw, kraw, vraw, qe, ka, kt, va, vt, qst, qraw_t, qrec, w, ot, ef, sp, sgt, doa, dss, dk, dv,
    dqb, dkb, dvb, hsend, hrecv, hot_c, hot_t, rsb, zb, pbb, agb, mysc,
    kv_s, kv_r, q_s, q_r, h_s, h_r, e_s, e_r, x_s, x_r, c_s, c_r, loc,
    rs_s, rs_r, z_s, z_r, p_s, p_r, a_s, a_r,
    gq_s, gq_r, bh_s, bh_r, bk_s, bk_r,
):
    me = lax.axis_index("seq")
    pb = lax.axis_index("pb")
    z = me // NY
    y = me % NY
    up = (z + 1) % NZ
    down = (z + NZ - 1) % NZ
    sibling = pb + 1 - 2 * (pb % 2)

    def at(zz, yy):
        return {"seq": zz * NY + yy, "pb": pb}

    def remote(src, dst, ss, rs, dev):
        return pltpu.make_async_remote_copy(
            src_ref=src, dst_ref=dst, send_sem=ss, recv_sem=rs, device_id=dev, device_id_type=MESH
        )

    barrier = pltpu.get_barrier_semaphore()

    def greet(dev):
        pl.semaphore_signal(barrier, inc=1, device_id=dev, device_id_type=MESH)

    for k in range(1, NY):
        greet(at(z, (y + k) % NY))
    for k in range(1, NZ):
        greet(at((z + k) % NZ, y))
    for k in range(1, NPB):
        greet({"seq": me, "pb": (pb + k) % NPB})
    for zi in range(2):
        for yi in range(NY):
            source_z = 2 * y + zi

            @pl.when(jnp.logical_or(source_z != z, yi != y))
            def _():
                greet(at(source_z, yi))

    e_yy = z // 2
    e_self = (e_yy == y).astype(jnp.int32)
    pl.semaphore_wait(barrier, (NY - 1) + (NZ - 1) + (NPB - 1) + NZ - e_self)

    def kv_copy(dy, g, which):
        src, dst = (k_ref, kraw) if which == 0 else (v_ref, vraw)
        ty = (y + dy) % NY
        return remote(
            src.at[:, aligned(ty * 256 + g * 128, 128)],
            dst.at[aligned(ROWS + y * BLOCK, BLOCK), pl.ds(g * 128, 128)],
            kv_s.at[dy - 1, g, which],
            kv_r.at[dy - 1, g, which],
            at(z, ty),
        )

    def kv_landed(dy, g, which):
        src, dst = (k_ref, kraw) if which == 0 else (v_ref, vraw)
        sy = (y + NY - dy) % NY
        return remote(
            src.at[:, aligned(y * 256 + g * 128, 128)],
            dst.at[aligned(ROWS + sy * BLOCK, BLOCK), pl.ds(g * 128, 128)],
            kv_s.at[dy - 1, g, which],
            kv_r.at[dy - 1, g, which],
            at(z, sy),
        )

    def q_copy(dy, g):
        ty = (y + dy) % NY
        return remote(
            q_ref.at[:, aligned(ty * 1024 + g * 512, 512)],
            qraw.at[aligned(y * BLOCK, BLOCK), aligned(g * 512, 512)],
            q_s.at[dy - 1, g],
            q_r.at[dy - 1, g],
            at(z, ty),
        )

    def q_landed(dy, g):
        sy = (y + NY - dy) % NY
        return remote(
            q_ref.at[:, aligned(y * 1024 + g * 512, 512)],
            qraw.at[aligned(sy * BLOCK, BLOCK), aligned(g * 512, 512)],
            q_s.at[dy - 1, g],
            q_r.at[dy - 1, g],
            at(z, sy),
        )

    own_rows = aligned(ROWS + y * BLOCK, BLOCK)
    local = [
        pltpu.make_async_copy(k_ref.at[:, aligned(y * 256, 256)], kraw.at[own_rows, :], loc.at[0]),
        pltpu.make_async_copy(v_ref.at[:, aligned(y * 256, 256)], vraw.at[own_rows, :], loc.at[1]),
        pltpu.make_async_copy(
            q_ref.at[:, aligned(y * 1024, 1024)], qraw.at[aligned(y * BLOCK, BLOCK), :], loc.at[2]
        ),
        pltpu.make_async_copy(
            e_ref, qe.at[pb, :, aligned((z % 2) * 512 + y * 128, 128)], loc.at[3]
        ),
    ]
    local[0].start()
    local[1].start()
    order = (2, 1, 3)
    for g in range(2):
        for which in range(2):
            for dy in order:
                kv_copy(dy, g, which).start()
    local[2].start()

    def e_copy(k):
        tz = (z + k) % NZ
        col = aligned((z % 2) * 512 + y * 128, 128)
        return remote(e_ref, qe.at[pb, :, col], e_s.at[k], e_r.at[z % 2, y], at(tz, e_yy))

    @pl.when(e_self == 1)
    def _():
        local[3].start()

    for k in range(NZ):
        if k == 0:

            @pl.when(e_self == 0)
            def _():
                e_copy(0).start()
        else:
            e_copy(k).start()

    for g in range(2):
        for dy in order:
            q_copy(dy, g).start()

    dfirst_r, dend_r, dfirst_c, dend_c = segments(dlen_ref[...])
    sfirst_r, send_r, sfirst_c, send_c = segments(slen_ref[...])
    span_col = column(slen_ref[...])[:, :1]
    qgain_col = column(qgain_ref[...])[:, :1]
    kgain = kgain_ref[...]
    base = z * ROWS
    tok_c = (base + iota((SPANS, ROWS), 1)).astype(F32)
    hot_c[...] = jnp.where(
        jnp.logical_and(tok_c >= sfirst_c, tok_c < send_c), 1.0, 0.0
    ).astype(BF16)
    tok_k = base - ROWS + iota((3 * ROWS, 128), 0)
    tok_kf = tok_k.astype(F32)
    lane_k = iota((3 * ROWS, 128), 1)
    same = jnp.logical_and(tok_kf >= dfirst_r, tok_kf < dend_r)
    outside = jnp.logical_and(
        lane_k == 127, jnp.logical_or(tok_k < 0, tok_k >= NZ * ROWS)
    )
    kdoc = jnp.where(jnp.logical_or(same, outside), 1.0, 0.0).astype(BF16)
    ones_v = jnp.where(lane_k < 3, 1.0, 0.0).astype(BF16)
    for g in range(2):
        ka[g, :, 128:256] = kdoc
        va[g, :, 128:256] = ones_v
    tok_q = (base + iota((128, ROWS), 1)).astype(F32)
    hot_t[...] = jnp.where(
        jnp.logical_and(tok_q >= dfirst_c, tok_q < dend_c), 0.0, -MASKED
    ).astype(BF16)
    sp[...] = jnp.zeros_like(sp)

    def halo(b, g, which, direction):
        buf = kraw if which == 0 else vraw
        cols = pl.ds(g * 128, 128)
        dst_row = b * BLOCK + (0 if direction == 0 else 2 * ROWS)
        return remote(
            buf.at[aligned(ROWS + b * BLOCK, BLOCK), cols],
            buf.at[aligned(dst_row, BLOCK), cols],
            h_s.at[b, g, which, direction],
            h_r.at[b, g, which, direction],
            at(up if direction == 0 else down, y),
        )

    local[0].wait()
    local[1].wait()
    for g in range(2):
        for which in range(2):
            for direction in range(2):
                halo(y, g, which, direction).start()
        for dy in (1, 3, 2):
            for which in range(2):
                kv_landed(dy, g, which).wait_recv()
                for direction in range(2):
                    halo((y + NY - dy) % NY, g, which, direction).start()

    @pl.when(e_self == 1)
    def _():
        local[3].wait()

    for zi in range(2):
        for yi in range(NY):

            @pl.when(jnp.logical_or(2 * y + zi != z, yi != y))
            def _():
                remote(
                    e_ref, qe.at[pb, :, pl.ds(zi * 512 + yi * 128, 128)], e_s.at[0],
                    e_r.at[zi, yi], at(2 * y + zi, yi),
                ).wait_recv()

    def x_copy(k):
        return remote(
            qe.at[pb], qe.at[pb], x_s.at[k - 1], x_r.at[k - 1],
            {"seq": me, "pb": (pb + 2 * k) % NPB},
        )

    def x_landed(k):
        src = (pb + NPB - 2 * k) % NPB
        return remote(
            qe.at[src], qe.at[src], x_s.at[k - 1], x_r.at[k - 1], {"seq": me, "pb": src}
        )

    def c_copy(k):
        part = (pb + NPB - 2 * k) % NPB
        return remote(
            qe.at[part], qe.at[part], c_s.at[k], c_r.at[k], {"seq": me, "pb": sibling}
        )

    def c_landed(k):
        part = (sibling + NPB - 2 * k) % NPB
        return remote(
            qe.at[part], qe.at[part], c_s.at[k], c_r.at[k], {"seq": me, "pb": sibling}
        )

    for k in (2, 1, 3):
        x_copy(k).start()
    c_copy(0).start()

    local[2].wait()
    def forward_group(g, _):
        for b in range(NY):
            for which in range(2):
                for direction in range(2):
                    halo(b, g, which, direction).wait_recv()
        cols = aligned(g * 128, 128)
        key = kraw[:, cols].astype(F32)
        rec = lax.rsqrt(jnp.mean(key * key, axis=1, keepdims=True) + EPS)
        key = key * rec * kgain
        ka[g, :, 0:128] = key.astype(BF16)
        kt[g] = jnp.transpose(key).astype(BF16)
        val = vraw[:, cols]
        va[g, :, 0:128] = val
        vt[g] = jnp.transpose(val.astype(F32)).astype(BF16)

        def tile(i, _):
            r = (y + i) % NY

            @pl.when(i != 0)
            def _():
                q_landed(NY - i, g).wait_recv()

            idx = g * NY + r
            rows = aligned(r * BLOCK, BLOCK)
            x = qraw[rows, aligned(g * 512, 512)].astype(F32)
            x = jnp.concatenate(
                [jnp.transpose(x[:, h * 128 : (h + 1) * 128]) for h in range(4)], axis=1
            )
            qraw_t[idx] = x.astype(BF16)
            rq = lax.rsqrt(jnp.mean(x * x, axis=0, keepdims=True) + EPS)
            qrec[idx] = rq
            qst[idx, 0:128, :] = (x * rq * qgain_col).astype(BF16)
            qdoc = hot_t[:, rows]
            qst[idx, 128:256, :] = jnp.concatenate([qdoc] * 4, axis=1)
            rhs = qst[idx]
            total = jnp.zeros((1, 512), F32)
            for c in range(WINDOW // CHUNK):
                part = slice(c * CHUNK, (c + 1) * CHUNK)
                s = dot(ka[g, aligned(r * BLOCK + c * CHUNK, CHUNK), :], rhs)
                e = jnp.exp2(s * (LOG2E * SCALE))
                total = total + jnp.sum(e, axis=0, keepdims=True)
                ef[part, :] = e
            inv = 1.0 / total
            for c in range(WINDOW // CHUNK):
                part = slice(c * CHUNK, (c + 1) * CHUNK)
                w[idx, part, :] = (ef[part, :] * inv).astype(BF16)
            out = dot(vt[g, :, aligned(r * BLOCK, WINDOW)], w[idx]).astype(BF16)
            ot[idx] = out
            table = hot_c[:, rows]
            for h in range(4):
                hc = aligned(g * 512 + h * 128, 128)
                sp[:, hc] += dot_nt(table, out[:, h * 128 : (h + 1) * 128])
            return 0

        lax.fori_loop(0, NY, tile, 0)
        return 0

    lax.fori_loop(0, 2, forward_group, 0)

    for k in range(1, 4):
        x_landed(k).wait_recv()
        c_copy(k).start()
    for k in range(4):
        c_landed(k).wait_recv()

    emb = qe[...].reshape(QUERIES, 1024)
    span = (sp[...] / span_col).astype(BF16)
    sims = dot_nt(span, emb)
    mine = ans_ref[...] - pb * SPANS
    span_no = iota((SPANS, QUERIES), 0)
    for j in range(CAND):
        mysc[j : j + 1, :] = jnp.sum(
            jnp.where(span_no == mine[j : j + 1, :], sims, 0.0), axis=0, keepdims=True
        )

    def lanes(t):
        return aligned(t * 128, 128)

    def rs_copy(dy):
        ty = (y + dy) % NY
        return remote(mysc.at[:, lanes(ty)], rsb.at[y], rs_s.at[dy - 1], rs_r.at[dy - 1], at(z, ty))

    def rs_landed(dy):
        sy = (y + NY - dy) % NY
        return remote(mysc.at[:, lanes(y)], rsb.at[sy], rs_s.at[dy - 1], rs_r.at[dy - 1], at(z, sy))

    def z_copy(k):
        return remote(zb.at[z], zb.at[z], z_s.at[k - 1], z_r.at[k - 1], at((z + k) % NZ, y))

    def z_landed(k):
        src = (z + NZ - k) % NZ
        return remote(zb.at[src], zb.at[src], z_s.at[k - 1], z_r.at[k - 1], at(src, y))

    def p_copy(k):
        return remote(
            pbb.at[pb], pbb.at[pb], p_s.at[k - 1], p_r.at[k - 1],
            {"seq": me, "pb": (pb + k) % NPB},
        )

    def p_landed(k):
        src = (pb + NPB - k) % NPB
        return remote(
            pbb.at[src], pbb.at[src], p_s.at[k - 1], p_r.at[k - 1], {"seq": me, "pb": src}
        )

    def a_copy(dy):
        ty = (y + dy) % NY
        return remote(agb.at[y], agb.at[y], a_s.at[dy - 1], a_r.at[dy - 1], at(z, ty))

    def a_landed(dy):
        sy = (y + NY - dy) % NY
        return remote(agb.at[sy], agb.at[sy], a_s.at[dy - 1], a_r.at[dy - 1], at(z, sy))

    for dy in order:
        rs_copy(dy).start()
    rsb[y] = mysc[:, lanes(y)]
    for dy in order:
        rs_landed(dy).wait_recv()
    part = rsb[0]
    for t in range(1, NY):
        part = part + rsb[t]
    zb[z] = part
    for k in (4, 3, 5, 2, 6, 1, 7):
        z_copy(k).start()
    for k in range(1, NZ):
        z_landed(k).wait_recv()
    part = zb[0]
    for t in range(1, NZ):
        part = part + zb[t]
    pbb[pb] = part
    for k in (4, 3, 5, 2, 6, 1, 7):
        p_copy(k).start()
    for k in range(1, NPB):
        p_landed(k).wait_recv()
    part = pbb[0]
    for t in range(1, NPB):
        part = part + pbb[t]
    agb[y] = part
    for dy in order:
        a_copy(dy).start()
    for dy in order:
        a_landed(dy).wait_recv()
    sims = jnp.concatenate([agb[t] for t in range(NY)], axis=1) / 0.05
    ex = jnp.exp(sims)
    den = jnp.sum(ex, axis=0, keepdims=True)
    loss = jnp.log(den) - sims[0:1, :]
    own_loss = jnp.zeros((1, QUERIES // NPB), F32)
    for t in range(NPB):
        size = QUERIES // NPB
        own_loss = jnp.where(pb == t, loss[:, t * size : (t + 1) * size], own_loss)
    loss_ref[...] = own_loss
    hit = (iota((CAND, QUERIES), 0) == 0).astype(F32)
    weight = 256.0 * (ex / den - hit) / 0.05
    dense = jnp.zeros((SPANS, QUERIES), F32)
    for j in range(CAND):
        dense = dense + jnp.where(span_no == mine[j : j + 1, :], weight[j : j + 1, :], 0.0)
    high = dense.astype(BF16)
    low = (dense - high.astype(F32)).astype(BF16)
    sg = (dot(high, emb) + dot(low, emb)) / span_col
    for h in range(8):
        cols = slice(h * 128, (h + 1) * 128)
        sgt[cols, :] = jnp.transpose(sg[:, cols]).astype(BF16)

    def gq_copy(g, r, slot):
        return remote(
            dqb.at[aligned(r * BLOCK, BLOCK), aligned(g * 512, 512)],
            gq_ref.at[:, aligned(y * 1024 + g * 512, 512)],
            gq_s.at[slot, g],
            gq_r.at[slot, g],
            at(z, r),
        )

    def gq_landed(g, r, slot):
        return remote(
            dqb.at[aligned(r * BLOCK, BLOCK), aligned(g * 512, 512)],
            gq_ref.at[:, aligned(r * 1024 + g * 512, 512)],
            gq_s.at[slot, g],
            gq_r.at[slot, g],
            at(z, r),
        )

    def gq_local(g):
        return pltpu.make_async_copy(
            dqb.at[aligned(y * BLOCK, BLOCK), aligned(g * 512, 512)],
            gq_ref.at[:, aligned(y * 1024 + g * 512, 512)],
            loc.at[4 + g],
        )

    def back_halo(g, which, direction):
        return remote(
            hsend.at[direction, g, which],
            hrecv.at[direction, g, which],
            bh_s.at[direction, g, which],
            bh_r.at[direction, g, which],
            at(down if direction == 0 else up, y),
        )

    def backward_group(g, _):
        dk[g] = jnp.zeros((3 * ROWS, 128), F32)
        dv[g] = jnp.zeros((3 * ROWS, 128), F32)

        def tile(i, _):
            off = jnp.where(i == 0, 2, jnp.where(i == 1, 1, jnp.where(i == 2, 3, 0)))
            r = (y + off) % NY
            idx = g * NY + r
            rows = aligned(r * BLOCK, BLOCK)
            go = dot(sgt[aligned(g * 512, 512), :], hot_c[:, rows])
            go = jnp.concatenate([go[h * 128 : (h + 1) * 128, :] for h in range(4)], axis=1)
            gob = go.astype(BF16)
            delta = jnp.sum(go * ot[idx].astype(F32), axis=0, keepdims=True)
            d0 = delta.astype(BF16).astype(F32)
            d1 = (delta - d0).astype(BF16).astype(F32)
            d2 = delta - d0 - d1
            row = iota((128, 512), 0)
            extra = jnp.where(row == 0, -d0, jnp.where(row == 1, -d1, jnp.where(row == 2, -d2, 0.0)))
            doa[0:128, :] = gob
            doa[128:256, :] = extra.astype(BF16)
            rhs = doa[...]
            for c in range(WINDOW // CHUNK):
                dp = dot(va[g, aligned(r * BLOCK + c * CHUNK, CHUNK), :], rhs)
                part = slice(c * CHUNK, (c + 1) * CHUNK)
                dss[part, :] = (w[idx, part, :].astype(F32) * dp).astype(BF16)
            window = aligned(r * BLOCK, WINDOW)
            dv[g, window, :] += dot_nt(w[idx], gob)
            dk[g, window, :] += dot_nt(dss[...], qst[idx, 0:128, :])
            dq = dot(kt[g, :, window], dss[...])
            x = qraw_t[idx].astype(F32)
            rq = qrec[idx]
            gained = (qgain_col * SCALE) * dq
            mean = jnp.mean(x * gained, axis=0, keepdims=True)
            res = rq * gained - x * (rq * rq * rq * mean)
            for h in range(4):
                dqb[rows, aligned(g * 512 + h * 128, 128)] = jnp.transpose(
                    res[:, h * 128 : (h + 1) * 128]
                ).astype(BF16)

            @pl.when(i != 3)
            def _():
                gq_copy(g, r, i).start()

            @pl.when(i == 3)
            def _():
                gq_local(g).start()

            return 0

        lax.fori_loop(0, NY, tile, 0)
        hsend[0, g, 0] = (dk[g, 0:ROWS, :] * SCALE).astype(BF16)
        hsend[0, g, 1] = dv[g, 0:ROWS, :].astype(BF16)
        hsend[1, g, 0] = (dk[g, 2 * ROWS : 3 * ROWS, :] * SCALE).astype(BF16)
        hsend[1, g, 1] = dv[g, 2 * ROWS : 3 * ROWS, :].astype(BF16)
        for which in range(2):
            for direction in range(2):
                back_halo(g, which, direction).start()
        return 0

    lax.fori_loop(0, 2, backward_group, 0)

    def bk_copy(dy, g, which):
        ty = (y + dy) % NY
        src, dst = (dkb, gk_ref) if which == 0 else (dvb, gv_ref)
        return remote(
            src.at[aligned(ty * BLOCK, BLOCK), pl.ds(g * 128, 128)],
            dst.at[:, aligned(y * 256 + g * 128, 128)],
            bk_s.at[dy - 1, g, which],
            bk_r.at[dy - 1, g, which],
            at(z, ty),
        )

    def bk_landed(dy, g, which):
        sy = (y + NY - dy) % NY
        src, dst = (dkb, gk_ref) if which == 0 else (dvb, gv_ref)
        return remote(
            src.at[aligned(sy * BLOCK, BLOCK), pl.ds(g * 128, 128)],
            dst.at[:, aligned(sy * 256 + g * 128, 128)],
            bk_s.at[dy - 1, g, which],
            bk_r.at[dy - 1, g, which],
            at(z, sy),
        )

    def bk_local(g, which):
        src, dst = (dkb, gk_ref) if which == 0 else (dvb, gv_ref)
        return pltpu.make_async_copy(
            src.at[aligned(y * BLOCK, BLOCK), pl.ds(g * 128, 128)],
            dst.at[:, aligned(y * 256 + g * 128, 128)],
            loc.at[6 + 2 * g + which],
        )

    for g in range(2):
        cols = slice(g * 128, (g + 1) * 128)
        for direction in range(2):
            for which in range(2):
                back_halo(g, which, direction).wait_recv()
        vtot = dv[g, ROWS : 2 * ROWS, :] + hrecv[0, g, 1].astype(F32) + hrecv[1, g, 1].astype(F32)
        dvb[:, cols] = vtot.astype(BF16)
        for dy in order:
            bk_copy(dy, g, 1).start()
        bk_local(g, 1).start()
        ktot = (
            dk[g, ROWS : 2 * ROWS, :] * SCALE
            + hrecv[0, g, 0].astype(F32)
            + hrecv[1, g, 0].astype(F32)
        )
        x = kraw[ROWS : 2 * ROWS, cols].astype(F32)
        rec = lax.rsqrt(jnp.mean(x * x, axis=1, keepdims=True) + EPS)
        gained = kgain * ktot
        mean = jnp.mean(x * gained, axis=1, keepdims=True)
        dkb[:, cols] = (rec * gained - x * (rec * rec * rec * mean)).astype(BF16)
        for dy in order:
            bk_copy(dy, g, 0).start()
        bk_local(g, 0).start()

    for g in range(2):
        gq_local(g).wait()
        for slot, off in enumerate((2, 1, 3)):
            gq_copy(g, (y + off) % NY, slot).wait_send()
            gq_landed(g, (y + NY - off) % NY, slot).wait_recv()
            q_copy(off, g).wait_send()
        for which in range(2):
            bk_local(g, which).wait()
            for dy in order:
                bk_copy(dy, g, which).wait_send()
                bk_landed(dy, g, which).wait_recv()
                kv_copy(dy, g, which).wait_send()
            for direction in range(2):
                back_halo(g, which, direction).wait_send()
                for b in range(NY):
                    halo(b, g, which, direction).wait_send()
    for dy in order:
        rs_copy(dy).wait_send()
        a_copy(dy).wait_send()
        x_copy(dy).wait_send()
    for k in range(4):
        c_copy(k).wait_send()
    for k in range(1, NZ):
        z_copy(k).wait_send()
        p_copy(k).wait_send()
        e_copy(k).wait_send()

    @pl.when(e_self == 0)
    def _():
        e_copy(0).wait_send()


def on_device(
    queries, keys, values, query_gain, key_gain, doc_lengths, span_lengths, query_emb, answer_options
):
    dlen = jnp.pad(doc_lengths.astype(F32), ((0, 0), (0, 128 - doc_lengths.shape[1])))
    slen = span_lengths.astype(F32)
    anywhere = pl.BlockSpec(memory_space=pl.ANY)
    vmem = pl.BlockSpec(memory_space=pltpu.VMEM)

    def dma(*shape):
        return pltpu.SemaphoreType.DMA(shape)

    tok = BLOCK
    loss, gq, gk, gv = pl.pallas_call(
        body,
        out_shape=(
            jax.ShapeDtypeStruct((1, QUERIES // NPB), F32),
            jax.ShapeDtypeStruct((tok, 4096), BF16),
            jax.ShapeDtypeStruct((tok, 1024), BF16),
            jax.ShapeDtypeStruct((tok, 1024), BF16),
        ),
        in_specs=[anywhere] * 4 + [vmem] * 5,
        out_specs=(vmem, anywhere, anywhere, anywhere),
        scratch_shapes=[
            pltpu.VMEM((ROWS, 1024), BF16),
            pltpu.VMEM((3 * ROWS, 256), BF16),
            pltpu.VMEM((3 * ROWS, 256), BF16),
            pltpu.VMEM((NPB, QUERIES // NPB, 1024), BF16),
            pltpu.VMEM((2, 3 * ROWS, 256), BF16),
            pltpu.VMEM((2, 128, 3 * ROWS), BF16),
            pltpu.VMEM((2, 3 * ROWS, 256), BF16),
            pltpu.VMEM((2, 128, 3 * ROWS), BF16),
            pltpu.VMEM((8, 256, 512), BF16),
            pltpu.VMEM((8, 128, 512), BF16),
            pltpu.VMEM((8, 1, 512), F32),
            pltpu.VMEM((8, WINDOW, 512), BF16),
            pltpu.VMEM((8, 128, 512), BF16),
            pltpu.VMEM((WINDOW, 512), F32),
            pltpu.VMEM((SPANS, 1024), F32),
            pltpu.VMEM((1024, SPANS), BF16),
            pltpu.VMEM((256, 512), BF16),
            pltpu.VMEM((WINDOW, 512), BF16),
            pltpu.VMEM((2, 3 * ROWS, 128), F32),
            pltpu.VMEM((2, 3 * ROWS, 128), F32),
            pltpu.VMEM((ROWS, 1024), BF16),
            pltpu.VMEM((ROWS, 256), BF16),
            pltpu.VMEM((ROWS, 256), BF16),
            pltpu.VMEM((2, 2, 2, ROWS, 128), BF16),
            pltpu.VMEM((2, 2, 2, ROWS, 128), BF16),
            pltpu.VMEM((SPANS, ROWS), BF16),
            pltpu.VMEM((128, ROWS), BF16),
            pltpu.VMEM((NY, 8, 128), F32),
            pltpu.VMEM((NZ, 8, 128), F32),
            pltpu.VMEM((NPB, 8, 128), F32),
            pltpu.VMEM((NY, 8, 128), F32),
            pltpu.VMEM((CAND, QUERIES), F32),
            dma(3, 2, 2), dma(3, 2, 2),
            dma(3, 2), dma(3, 2),
            dma(NY, 2, 2, 2), dma(NY, 2, 2, 2),
            dma(NZ), dma(2, NY),
            dma(3), dma(3),
            dma(4), dma(4),
            dma(10),
            dma(3), dma(3),
            dma(7), dma(7),
            dma(7), dma(7),
            dma(3), dma(3),
            dma(3, 2), dma(3, 2),
            dma(2, 2, 2), dma(2, 2, 2),
            dma(3, 2, 2), dma(3, 2, 2),
        ],
        compiler_params=pltpu.CompilerParams(
            collective_id=0, has_side_effects=True, vmem_limit_bytes=56 * 1024 * 1024
        ),
        cost_estimate=pl.CostEstimate(
            flops=8 * 6 * 2 * WINDOW * 512 * 128, bytes_accessed=3 << 20, transcendentals=8 * WINDOW * 512
        ),
        name="attention_contrastive",
    )(
        queries[0],
        keys[0],
        values[0],
        query_emb,
        query_gain.reshape(1, 128),
        key_gain.reshape(1, 128),
        dlen,
        slen,
        answer_options.T,
    )
    return loss.reshape(QUERIES // NPB), gq[None], gk[None], gv[None]


def solution(mesh):
    in_specs = (
        P("pb", "seq", None),
        P("pb", "seq", None),
        P("pb", "seq", None),
        P(),
        P(),
        P("pb", None),
        P("pb", None),
        P("pb", "seq"),
        P(),
    )
    out_specs = (P("pb"), P("pb", "seq", None), P("pb", "seq", None), P("pb", "seq", None))
    return jax.shard_map(
        on_device, mesh=mesh, in_specs=in_specs, out_specs=out_specs, check_vma=False
    )
```

```python
import functools
import math

import jax
import jax.numpy as jnp
from jax import lax
from jax.experimental import pallas as pl
from jax.experimental.pallas import tpu as pltpu
from jax.sharding import PartitionSpec as P

WIDTH = 128
NY = 4
NZ = 8
NPB = 8
BLOCK = 128
ROWS = 512
WINDOW = 1152
CHUNK = 384
SPANS = 128
QUERIES = 512
CAND = 8
EPS = 1e-06
MASKED = 16384.0
LOG2E = math.log2(math.e)
SCALE = 1.0 / math.sqrt(WIDTH)
F32 = jnp.float32
BF16 = jnp.bfloat16
MESH = pl.DeviceIdType.MESH
NT = (((1,), (1,)), ((), ()))


def dot(a, b):
    return jnp.dot(a, b, preferred_element_type=F32)


def dot_nt(a, b):
    return lax.dot_general(a, b, NT, preferred_element_type=F32)


def turned(x):
    return jnp.transpose(x.astype(F32))


def iota(shape, dim):
    return lax.broadcasted_iota(jnp.int32, shape, dim)


def aligned(start, size, unit=128):
    return pl.ds(pl.multiple_of(start, unit), size)


def column(row):
    return jnp.transpose(jnp.broadcast_to(row, (128, 128)))


def segments(lens):
    down = column(lens)
    across = jnp.broadcast_to(lens, (128, 128))
    sub, lane = iota((128, 128), 0), iota((128, 128), 1)
    first_row = jnp.sum(jnp.where(sub < lane, down, 0.0), axis=0, keepdims=True)
    first_col = jnp.sum(jnp.where(lane < sub, across, 0.0), axis=1, keepdims=True)
    return first_row, first_row + lens, first_col, first_col + down[:, :1]


def body(
    q_ref, k_ref, v_ref, e_ref, qgain_ref, kgain_ref, dlen_ref, slen_ref, ans_ref,
    loss_ref, gq_ref, gk_ref, gv_ref,
    qraw, kraw, vraw, qe, ka, kt, va, vt, qst, qraw_t, qrec, w, ot, ef, sp, sgt, doa, dss, dk, dv,
    dqb, dkb, dvb, hsend, hrecv, hot_c, rsb, zb, pbb, agb, mysc, dli, sli, qgi, kgi, ansi,
    kv_s, kv_r, q_s, q_r, h_s, h_r, e_s, e_r, x_s, x_r, c_s, c_r, loc,
    rs_s, rs_r, z_s, z_r, p_s, p_r, a_s, a_r,
    gq_s, gq_r, bh_s, bh_r, bk_s, bk_r,
):
    me = lax.axis_index("seq")
    pb = lax.axis_index("pb")
    z = me // NY
    y = me % NY
    up = (z + 1) % NZ
    down = (z + NZ - 1) % NZ
    sibling = pb + 1 - 2 * (pb % 2)

    def at(zz, yy):
        return {"seq": zz * NY + yy, "pb": pb}

    def remote(src, dst, ss, rs, dev):
        return pltpu.make_async_remote_copy(
            src_ref=src, dst_ref=dst, send_sem=ss, recv_sem=rs, device_id=dev, device_id_type=MESH
        )

    small = [
        pltpu.make_async_copy(src, dst, loc.at[10 + i])
        for i, (src, dst) in enumerate(
            ((dlen_ref, dli), (slen_ref, sli), (qgain_ref, qgi), (kgain_ref, kgi), (ans_ref, ansi))
        )
    ]
    for copy in small:
        copy.start()

    barrier = pltpu.get_barrier_semaphore()

    def greet(dev):
        pl.semaphore_signal(barrier, inc=1, device_id=dev, device_id_type=MESH)

    for k in range(1, NY):
        greet(at(z, (y + k) % NY))
    for k in range(1, NZ):
        greet(at((z + k) % NZ, y))
    for k in range(1, NPB):
        greet({"seq": me, "pb": (pb + k) % NPB})
    for zi in range(2):
        for k in range(1, NY):

            @pl.when(2 * y + zi != z)
            def _():
                greet(at(2 * y + zi, (y + k) % NY))

    e_yy = z // 2
    e_self = (e_yy == y).astype(jnp.int32)
    pl.semaphore_wait(barrier, NY + NZ + NPB - 3 + jnp.where(e_self == 1, 0, NZ - 1))

    def kv_copy(dy, g, which):
        src, dst = (k_ref, kraw) if which == 0 else (v_ref, vraw)
        ty = (y + dy) % NY
        return remote(
            src.at[:, aligned(ty * 256 + g * 128, 128)],
            dst.at[aligned(ROWS + y * BLOCK, BLOCK), pl.ds(g * 128, 128)],
            kv_s.at[dy - 1, g, which],
            kv_r.at[dy - 1, g, which],
            at(z, ty),
        )

    def kv_landed(dy, g, which):
        src, dst = (k_ref, kraw) if which == 0 else (v_ref, vraw)
        sy = (y + NY - dy) % NY
        return remote(
            src.at[:, aligned(y * 256 + g * 128, 128)],
            dst.at[aligned(ROWS + sy * BLOCK, BLOCK), pl.ds(g * 128, 128)],
            kv_s.at[dy - 1, g, which],
            kv_r.at[dy - 1, g, which],
            at(z, sy),
        )

    def q_copy(dy, g):
        ty = (y + dy) % NY
        return remote(
            q_ref.at[:, aligned(ty * 1024 + g * 512, 512)],
            qraw.at[aligned(y * BLOCK, BLOCK), aligned(g * 512, 512)],
            q_s.at[dy - 1, g],
            q_r.at[dy - 1, g],
            at(z, ty),
        )

    def q_landed(dy, g):
        sy = (y + NY - dy) % NY
        return remote(
            q_ref.at[:, aligned(y * 1024 + g * 512, 512)],
            qraw.at[aligned(sy * BLOCK, BLOCK), aligned(g * 512, 512)],
            q_s.at[dy - 1, g],
            q_r.at[dy - 1, g],
            at(z, sy),
        )

    own_rows = aligned(ROWS + y * BLOCK, BLOCK)
    local = [
        pltpu.make_async_copy(k_ref.at[:, aligned(y * 256, 256)], kraw.at[own_rows, :], loc.at[0]),
        pltpu.make_async_copy(v_ref.at[:, aligned(y * 256, 256)], vraw.at[own_rows, :], loc.at[1]),
        pltpu.make_async_copy(
            q_ref.at[:, aligned(y * 1024, 1024)], qraw.at[aligned(y * BLOCK, BLOCK), :], loc.at[2]
        ),
        pltpu.make_async_copy(
            e_ref, qe.at[pb, :, aligned((z % 2) * 512 + y * 128, 128)], loc.at[3]
        ),
    ]
    local[0].start()
    local[1].start()
    order = (2, 1, 3)

    def kv_start(g):
        for which in range(2):
            for dy in order:
                kv_copy(dy, g, which).start()

    def q_start(g):
        for dy in order:
            q_copy(dy, g).start()

    kv_start(0)
    local[2].start()

    def halo(b, g, which, direction, own=False):
        buf = kraw if which == 0 else vraw
        cols = pl.ds(g * 128, 128)
        dst_row = b * BLOCK + (0 if direction == 0 else 2 * ROWS)
        if own:
            src = (k_ref if which == 0 else v_ref).at[:, aligned(y * 256 + g * 128, 128)]
        else:
            src = buf.at[aligned(ROWS + b * BLOCK, BLOCK), cols]
        return remote(
            src,
            buf.at[aligned(dst_row, BLOCK), cols],
            h_s.at[b, g, which, direction],
            h_r.at[b, g, which, direction],
            at(up if direction == 0 else down, y),
        )

    def own_halo(g, which, direction):
        return halo(y, g, which, direction, True)

    for which in range(2):
        for direction in range(2):
            own_halo(0, which, direction).start()

    def e_copy(k):
        tz = (z + k) % NZ
        col = aligned((z % 2) * 512 + y * 128, 128)
        return remote(e_ref, qe.at[pb, :, col], e_s.at[k], e_r.at[z % 2, y], at(tz, e_yy))

    @pl.when(e_self == 1)
    def _():
        local[3].start()

    for k in range(NZ):
        if k == 0:

            @pl.when(e_self == 0)
            def _():
                e_copy(0).start()
        else:
            e_copy(k).start()

    def forward_halos(g):
        for dy in (1, 3, 2):
            for which in range(2):
                kv_landed(dy, g, which).wait_recv()
                for direction in range(2):
                    halo((y + NY - dy) % NY, g, which, direction).start()

    def own_halos(g):
        for which in range(2):
            for direction in range(2):
                own_halo(g, which, direction).start()

    kv_start(1)
    forward_halos(0)
    q_start(0)

    @pl.when(e_self == 1)
    def _():
        local[3].wait()

    for zi in range(2):
        for yi in range(NY):

            @pl.when(jnp.logical_or(2 * y + zi != z, yi != y))
            def _():
                remote(
                    e_ref, qe.at[pb, :, pl.ds(zi * 512 + yi * 128, 128)], e_s.at[0],
                    e_r.at[zi, yi], at(2 * y + zi, yi),
                ).wait_recv()

    def x_copy(k):
        return remote(
            qe.at[pb], qe.at[pb], x_s.at[k - 1], x_r.at[k - 1],
            {"seq": me, "pb": (pb + 2 * k) % NPB},
        )

    def x_landed(k):
        src = (pb + NPB - 2 * k) % NPB
        return remote(
            qe.at[src], qe.at[src], x_s.at[k - 1], x_r.at[k - 1], {"seq": me, "pb": src}
        )

    def c_copy(k):
        part = (pb + NPB - 2 * k) % NPB
        return remote(
            qe.at[part], qe.at[part], c_s.at[k], c_r.at[k], {"seq": me, "pb": sibling}
        )

    def c_landed(k):
        part = (sibling + NPB - 2 * k) % NPB
        return remote(
            qe.at[part], qe.at[part], c_s.at[k], c_r.at[k], {"seq": me, "pb": sibling}
        )

    for k in (2, 1, 3):
        x_copy(k).start()
    c_copy(0).start()

    for copy in small:
        copy.wait()
    dlen = jnp.concatenate([dli[...].astype(F32), jnp.zeros((1, 112), F32)], axis=1)
    slen = sli[...].astype(F32)
    dfirst_r, dend_r, dfirst_c, dend_c = segments(dlen)
    sfirst_r, send_r, sfirst_c, send_c = segments(slen)
    span_col = column(slen)[:, :1]
    qgain_col = column(qgi[...])[:, :1]
    kgain = kgi[...]
    base = z * ROWS
    tok_c = (base + iota((SPANS, ROWS), 1)).astype(F32)
    hot_c[...] = jnp.where(
        jnp.logical_and(tok_c >= sfirst_c, tok_c < send_c), 1.0, 0.0
    ).astype(BF16)
    tok_k = base - ROWS + iota((3 * ROWS, 128), 0)
    tok_kf = tok_k.astype(F32)
    lane_k = iota((3 * ROWS, 128), 1)
    same = jnp.logical_and(tok_kf >= dfirst_r, tok_kf < dend_r)
    outside = jnp.logical_and(
        lane_k == 127, jnp.logical_or(tok_k < 0, tok_k >= NZ * ROWS)
    )
    kdoc = jnp.where(jnp.logical_or(same, outside), 1.0, 0.0).astype(BF16)
    ones_v = jnp.where(lane_k < 3, 1.0, 0.0).astype(BF16)
    for g in range(2):
        ka[g, :, 128:256] = kdoc
        va[g, :, 128:256] = ones_v
    tok_q = (base + iota((128, ROWS), 1)).astype(F32)
    qdoc = jnp.where(jnp.logical_and(tok_q >= dfirst_c, tok_q < dend_c), 0.0, -MASKED).astype(BF16)
    for r in range(NY):
        tile = jnp.concatenate([qdoc[:, r * BLOCK : (r + 1) * BLOCK]] * 4, axis=1)
        for g in range(2):
            qst[g * NY + r, 128:256, :] = tile
    doa[:, 128:256, :] = jnp.zeros((NY, 128, 512), BF16)
    sp[...] = jnp.zeros_like(sp)

    for copy in local[:3]:
        copy.wait()
    def forward_group(g):
        for b in range(NY):
            for which in range(2):
                for direction in range(2):
                    halo(b, g, which, direction).wait_recv()
        if g == 0:
            own_halos(1)
            forward_halos(1)
            q_start(1)
        cols = aligned(g * 128, 128)
        key = kraw[:, cols].astype(F32)
        square = key * key
        high = square.astype(BF16)
        low = (square - high.astype(F32)).astype(BF16)
        mean = dot(jnp.concatenate([high, low], axis=1), jnp.ones((256, 128), BF16)) * (1.0 / WIDTH)
        key = (key * lax.rsqrt(mean + EPS) * kgain).astype(BF16)
        ka[g, :, 0:128] = key
        kt[g] = turned(key).astype(BF16)
        val = vraw[:, cols]
        va[g, :, 0:128] = val
        vt[g] = turned(val).astype(BF16)

        def tile(i, _):
            r = (y + i) % NY

            @pl.when(i != 0)
            def _():
                q_landed(NY - i, g).wait_recv()

            idx = g * NY + r
            rows = aligned(r * BLOCK, BLOCK)
            x = qraw[rows, aligned(g * 512, 512)]
            x = jnp.concatenate(
                [turned(x[:, h * 128 : (h + 1) * 128]) for h in range(4)], axis=1
            )
            qraw_t[idx] = x.astype(BF16)
            rq = lax.rsqrt(jnp.mean(x * x, axis=0, keepdims=True) + EPS)
            qrec[idx] = rq
            qst[idx, 0:128, :] = (x * rq * qgain_col).astype(BF16)
            rhs = qst[idx]
            total = jnp.zeros((1, 512), F32)
            for c in range(WINDOW // CHUNK):
                part = slice(c * CHUNK, (c + 1) * CHUNK)
                s = dot(ka[g, aligned(r * BLOCK + c * CHUNK, CHUNK), :], rhs)
                e = jnp.exp2(s * (LOG2E * SCALE))
                total = total + jnp.sum(e, axis=0, keepdims=True)
                ef[part, :] = e
            inv = 1.0 / total
            for c in range(WINDOW // CHUNK):
                part = slice(c * CHUNK, (c + 1) * CHUNK)
                w[idx, part, :] = (ef[part, :] * inv).astype(BF16)
            out = dot(vt[g, :, aligned(r * BLOCK, WINDOW)], w[idx]).astype(BF16)
            ot[idx] = out
            table = hot_c[:, rows]
            for h in range(4):
                hc = aligned(g * 512 + h * 128, 128)
                sp[:, hc] += dot_nt(table, out[:, h * 128 : (h + 1) * 128])
            return 0

        lax.fori_loop(0, NY, tile, 0)

    forward_group(0)
    for k in range(1, 4):
        x_landed(k).wait_recv()
        c_copy(k).start()
    forward_group(1)
    for k in range(4):
        c_landed(k).wait_recv()

    emb = qe[...].reshape(QUERIES, 1024)
    span = (sp[...] / span_col).astype(BF16)
    sims = dot_nt(span, emb)
    mine = ansi[...] - pb * SPANS
    span_no = iota((SPANS, QUERIES), 0)
    for j in range(CAND):
        mysc[j : j + 1, :] = jnp.sum(
            jnp.where(span_no == mine[j : j + 1, :], sims, 0.0), axis=0, keepdims=True
        )

    def lanes(t):
        return aligned(t * 128, 128)

    def rs_copy(dy):
        ty = (y + dy) % NY
        return remote(mysc.at[:, lanes(ty)], rsb.at[y], rs_s.at[dy - 1], rs_r.at[dy - 1], at(z, ty))

    def rs_landed(dy):
        sy = (y + NY - dy) % NY
        return remote(mysc.at[:, lanes(y)], rsb.at[sy], rs_s.at[dy - 1], rs_r.at[dy - 1], at(z, sy))

    def z_copy(k):
        return remote(zb.at[z], zb.at[z], z_s.at[k - 1], z_r.at[k - 1], at((z + k) % NZ, y))

    def z_landed(k):
        src = (z + NZ - k) % NZ
        return remote(zb.at[src], zb.at[src], z_s.at[k - 1], z_r.at[k - 1], at(src, y))

    def p_copy(k):
        dev = {"seq": me, "pb": (pb + k) % NPB}
        return remote(pbb.at[pb], pbb.at[pb], p_s.at[k - 1], p_r.at[k - 1], dev)

    def p_landed(k):
        src = (pb + NPB - k) % NPB
        dev = {"seq": me, "pb": src}
        return remote(pbb.at[src], pbb.at[src], p_s.at[k - 1], p_r.at[k - 1], dev)

    def a_copy(dy):
        ty = (y + dy) % NY
        return remote(agb.at[y], agb.at[y], a_s.at[dy - 1], a_r.at[dy - 1], at(z, ty))

    def a_landed(dy):
        sy = (y + NY - dy) % NY
        return remote(agb.at[sy], agb.at[sy], a_s.at[dy - 1], a_r.at[dy - 1], at(z, sy))

    def total_of(buf, count):
        part = buf[0]
        for t in range(1, count):
            part = part + buf[t]
        return part

    far_first = (4, 3, 5, 2, 6, 1, 7)
    for dy in order:
        rs_copy(dy).start()
    rsb[y] = mysc[:, lanes(y)]
    for dy in order:
        rs_landed(dy).wait_recv()
    zb[z] = total_of(rsb, NY)
    for k in far_first:
        z_copy(k).start()
    for k in far_first:
        z_landed(k).wait_recv()
    pbb[pb] = total_of(zb, NZ)
    for k in far_first:
        p_copy(k).start()
    for k in far_first:
        p_landed(k).wait_recv()
    agb[y] = total_of(pbb, NPB)
    for dy in order:
        a_copy(dy).start()
    for dy in order:
        a_landed(dy).wait_recv()
    tiles = [agb[t] for t in range(NY)]
    sims = jnp.concatenate(tiles, axis=1) / 0.05
    ex = jnp.exp(sims)
    den = jnp.sum(ex, axis=0, keepdims=True)
    loss = jnp.log(den) - sims[0:1, :]
    own_loss = jnp.zeros((1, QUERIES // NPB), F32)
    for t in range(NPB):
        size = QUERIES // NPB
        own_loss = jnp.where(pb == t, loss[:, t * size : (t + 1) * size], own_loss)
    loss_ref[...] = own_loss
    hit = (iota((CAND, QUERIES), 0) == 0).astype(F32)
    weight = 256.0 * (ex / den - hit) / 0.05
    dense = jnp.zeros((SPANS, QUERIES), F32)
    for j in range(CAND):
        dense = dense + jnp.where(span_no == mine[j : j + 1, :], weight[j : j + 1, :], 0.0)
    high = dense.astype(BF16)
    low = (dense - high.astype(F32)).astype(BF16)
    sg = ((dot(high, emb) + dot(low, emb)) / span_col).astype(BF16)
    for h in range(8):
        cols = slice(h * 128, (h + 1) * 128)
        sgt[cols, :] = turned(sg[:, cols]).astype(BF16)

    def gq_copy(g, r, slot):
        return remote(
            dqb.at[aligned(r * BLOCK, BLOCK), aligned(g * 512, 512)],
            gq_ref.at[:, aligned(y * 1024 + g * 512, 512)],
            gq_s.at[slot, g],
            gq_r.at[slot, g],
            at(z, r),
        )

    def gq_landed(g, r, slot):
        return remote(
            dqb.at[aligned(r * BLOCK, BLOCK), aligned(g * 512, 512)],
            gq_ref.at[:, aligned(r * 1024 + g * 512, 512)],
            gq_s.at[slot, g],
            gq_r.at[slot, g],
            at(z, r),
        )

    def gq_local(g):
        return pltpu.make_async_copy(
            dqb.at[aligned(y * BLOCK, BLOCK), aligned(g * 512, 512)],
            gq_ref.at[:, aligned(y * 1024 + g * 512, 512)],
            loc.at[4 + g],
        )

    def back_halo(g, which, direction):
        return remote(
            hsend.at[direction, g, which],
            hrecv.at[direction, g, which],
            bh_s.at[direction, g, which],
            bh_r.at[direction, g, which],
            at(down if direction == 0 else up, y),
        )

    def send_halos(g, which, total, factor):
        for direction in range(2):
            first = 2 * ROWS * direction
            hsend[direction, g, which] = (total[g, first : first + ROWS, :] * factor).astype(BF16)
            back_halo(g, which, direction).start()

    def backward_group(g, _):
        dk[g] = jnp.zeros((3 * ROWS, 128), F32)
        dv[g] = jnp.zeros((3 * ROWS, 128), F32)

        def values_tile(r, _):
            idx = g * NY + r
            rows = aligned(r * BLOCK, BLOCK)
            go = dot(sgt[aligned(g * 512, 512), :], hot_c[:, rows])
            go = jnp.concatenate([go[h * 128 : (h + 1) * 128, :] for h in range(4)], axis=1)
            gob = go.astype(BF16)
            delta = jnp.sum(go * ot[idx].astype(F32), axis=0, keepdims=True)
            d0 = delta.astype(BF16).astype(F32)
            d1 = (delta - d0).astype(BF16).astype(F32)
            d2 = delta - d0 - d1
            row = iota((16, 512), 0)
            extra = jnp.where(row == 0, -d0, jnp.where(row == 1, -d1, jnp.where(row == 2, -d2, 0.0)))
            doa[r, 0:128, :] = gob
            doa[r, 128:144, :] = extra.astype(BF16)
            dv[g, aligned(r * BLOCK, WINDOW), :] += dot_nt(w[idx], gob)
            return 0

        lax.fori_loop(0, NY, values_tile, 0)
        send_halos(g, 1, dv, 1.0)

        def tile(i, _):
            off = jnp.where(i == 0, 2, jnp.where(i == 1, 1, jnp.where(i == 2, 3, 0)))
            r = (y + off) % NY
            idx = g * NY + r
            rows = aligned(r * BLOCK, BLOCK)
            rhs = doa[r]
            for c in range(WINDOW // CHUNK):
                dp = dot(va[g, aligned(r * BLOCK + c * CHUNK, CHUNK), :], rhs)
                part = slice(c * CHUNK, (c + 1) * CHUNK)
                dss[part, :] = (w[idx, part, :].astype(F32) * dp).astype(BF16)
            window = aligned(r * BLOCK, WINDOW)
            dk[g, window, :] += dot_nt(dss[...], qst[idx, 0:128, :])
            dq = dot(kt[g, :, window], dss[...])
            x = qraw_t[idx].astype(F32)
            rq = qrec[idx]
            gained = (qgain_col * SCALE) * dq
            mean = jnp.mean(x * gained, axis=0, keepdims=True)
            res = rq * gained - x * (rq * rq * rq * mean)
            for h in range(4):
                dqb[rows, aligned(g * 512 + h * 128, 128)] = turned(
                    res[:, h * 128 : (h + 1) * 128]
                ).astype(BF16)

            @pl.when(i != 3)
            def _():
                gq_copy(g, r, i).start()

            @pl.when(i == 3)
            def _():
                gq_local(g).start()

            return 0

        lax.fori_loop(0, NY, tile, 0)
        send_halos(g, 0, dk, SCALE)
        return 0

    lax.fori_loop(0, 2, backward_group, 0)

    def bk_copy(dy, g, which):
        ty = (y + dy) % NY
        src, dst = (dkb, gk_ref) if which == 0 else (dvb, gv_ref)
        return remote(
            src.at[aligned(ty * BLOCK, BLOCK), pl.ds(g * 128, 128)],
            dst.at[:, aligned(y * 256 + g * 128, 128)],
            bk_s.at[dy - 1, g, which],
            bk_r.at[dy - 1, g, which],
            at(z, ty),
        )

    def bk_landed(dy, g, which):
        sy = (y + NY - dy) % NY
        src, dst = (dkb, gk_ref) if which == 0 else (dvb, gv_ref)
        return remote(
            src.at[aligned(sy * BLOCK, BLOCK), pl.ds(g * 128, 128)],
            dst.at[:, aligned(sy * 256 + g * 128, 128)],
            bk_s.at[dy - 1, g, which],
            bk_r.at[dy - 1, g, which],
            at(z, sy),
        )

    def bk_local(g, which):
        src, dst = (dkb, gk_ref) if which == 0 else (dvb, gv_ref)
        return pltpu.make_async_copy(
            src.at[aligned(y * BLOCK, BLOCK), pl.ds(g * 128, 128)],
            dst.at[:, aligned(y * 256 + g * 128, 128)],
            loc.at[6 + 2 * g + which],
        )

    for g in range(2):
        cols = slice(g * 128, (g + 1) * 128)
        for direction in range(2):
            back_halo(g, 1, direction).wait_recv()
        vtot = dv[g, ROWS : 2 * ROWS, :] + hrecv[0, g, 1].astype(F32) + hrecv[1, g, 1].astype(F32)
        dvb[:, cols] = vtot.astype(BF16)
        for dy in order:
            bk_copy(dy, g, 1).start()
        bk_local(g, 1).start()
        for direction in range(2):
            back_halo(g, 0, direction).wait_recv()
        ktot = (
            dk[g, ROWS : 2 * ROWS, :] * SCALE
            + hrecv[0, g, 0].astype(F32)
            + hrecv[1, g, 0].astype(F32)
        )
        x = kraw[ROWS : 2 * ROWS, cols].astype(F32)
        rec = lax.rsqrt(jnp.mean(x * x, axis=1, keepdims=True) + EPS)
        gained = kgain * ktot
        mean = jnp.mean(x * gained, axis=1, keepdims=True)
        dkb[:, cols] = (rec * gained - x * (rec * rec * rec * mean)).astype(BF16)
        for dy in order:
            bk_copy(dy, g, 0).start()
        bk_local(g, 0).start()

    for g in range(2):
        gq_local(g).wait()
        for slot, off in enumerate((2, 1, 3)):
            gq_copy(g, (y + off) % NY, slot).wait_send()
            gq_landed(g, (y + NY - off) % NY, slot).wait_recv()
            q_copy(off, g).wait_send()
        for which in range(2):
            bk_local(g, which).wait()
            for dy in order:
                bk_copy(dy, g, which).wait_send()
                bk_landed(dy, g, which).wait_recv()
                kv_copy(dy, g, which).wait_send()
            for direction in range(2):
                back_halo(g, which, direction).wait_send()
                for b in range(NY):
                    halo(b, g, which, direction).wait_send()
    for dy in order:
        x_copy(dy).wait_send()
    for k in range(4):
        c_copy(k).wait_send()
    for k in range(1, NZ):
        e_copy(k).wait_send()

    for dy in order:
        rs_copy(dy).wait_send()
        a_copy(dy).wait_send()
    for k in far_first:
        z_copy(k).wait_send()
        p_copy(k).wait_send()

    @pl.when(e_self == 0)
    def _():
        e_copy(0).wait_send()


def hand_over(loss_in, gq_in, gk_in, gv_in, loss, gq, gk, gv, sem):
    copies = [
        pltpu.make_async_copy(src, dst, sem.at[i])
        for i, (src, dst) in enumerate(((gq_in, gq), (gk_in, gk), (gv_in, gv)))
    ]
    for copy in copies:
        copy.start()
    loss[...] = loss_in[0, :]
    for copy in copies:
        copy.wait()


def on_device(
    queries, keys, values, query_gain, key_gain, doc_lengths, span_lengths, query_emb, answer_options
):
    anywhere = pl.BlockSpec(memory_space=pl.ANY)
    vmem = pl.BlockSpec(memory_space=pltpu.VMEM)

    def dma(*shape):
        return pltpu.SemaphoreType.DMA(shape)

    tok = BLOCK
    loss, gq, gk, gv = pl.pallas_call(
        body,
        out_shape=(
            pltpu.VMEM((1, QUERIES // NPB), F32),
            pltpu.VMEM((tok, 4096), BF16),
            pltpu.VMEM((tok, 1024), BF16),
            pltpu.VMEM((tok, 1024), BF16),
        ),
        in_specs=[anywhere] * 9,
        out_specs=(vmem,) * 4,
        scratch_shapes=[
            pltpu.VMEM((ROWS, 1024), BF16),
            pltpu.VMEM((3 * ROWS, 256), BF16),
            pltpu.VMEM((3 * ROWS, 256), BF16),
            pltpu.VMEM((NPB, QUERIES // NPB, 1024), BF16),
            pltpu.VMEM((2, 3 * ROWS, 256), BF16),
            pltpu.VMEM((2, 128, 3 * ROWS), BF16),
            pltpu.VMEM((2, 3 * ROWS, 256), BF16),
            pltpu.VMEM((2, 128, 3 * ROWS), BF16),
            pltpu.VMEM((8, 256, 512), BF16),
            pltpu.VMEM((8, 128, 512), BF16),
            pltpu.VMEM((8, 1, 512), F32),
            pltpu.VMEM((8, WINDOW, 512), BF16),
            pltpu.VMEM((8, 128, 512), BF16),
            pltpu.VMEM((WINDOW, 512), F32),
            pltpu.VMEM((SPANS, 1024), F32),
            pltpu.VMEM((1024, SPANS), BF16),
            pltpu.VMEM((NY, 256, 512), BF16),
            pltpu.VMEM((WINDOW, 512), BF16),
            pltpu.VMEM((2, 3 * ROWS, 128), F32),
            pltpu.VMEM((2, 3 * ROWS, 128), F32),
            pltpu.VMEM((ROWS, 1024), BF16),
            pltpu.VMEM((ROWS, 256), BF16),
            pltpu.VMEM((ROWS, 256), BF16),
            pltpu.VMEM((2, 2, 2, ROWS, 128), BF16),
            pltpu.VMEM((2, 2, 2, ROWS, 128), BF16),
            pltpu.VMEM((SPANS, ROWS), BF16),
            pltpu.VMEM((NY, 8, 128), F32),
            pltpu.VMEM((NZ, 8, 128), F32),
            pltpu.VMEM((NPB, 8, 128), F32),
            pltpu.VMEM((NY, 8, 128), F32),
            pltpu.VMEM((CAND, QUERIES), F32),
            pltpu.VMEM((1, 16), jnp.int32),
            pltpu.VMEM((1, SPANS), jnp.int32),
            pltpu.VMEM((1, 128), F32),
            pltpu.VMEM((1, 128), F32),
            pltpu.VMEM((CAND, QUERIES), jnp.int32),
            dma(3, 2, 2), dma(3, 2, 2),
            dma(3, 2), dma(3, 2),
            dma(NY, 2, 2, 2), dma(NY, 2, 2, 2),
            dma(NZ), dma(2, NY),
            dma(3), dma(3),
            dma(4), dma(4),
            dma(15),
            dma(3), dma(3),
            dma(7), dma(7),
            dma(7), dma(7),
            dma(3), dma(3),
            dma(3, 2), dma(3, 2),
            dma(2, 2, 2), dma(2, 2, 2),
            dma(3, 2, 2), dma(3, 2, 2),
        ],
        compiler_params=pltpu.CompilerParams(
            collective_id=0, has_side_effects=True, vmem_limit_bytes=56 * 1024 * 1024
        ),
        cost_estimate=pl.CostEstimate(
            flops=8 * 6 * 2 * WINDOW * 512 * 128, bytes_accessed=3 << 20, transcendentals=8 * WINDOW * 512
        ),
        name="attention_contrastive",
    )(
        queries[0],
        keys[0],
        values[0],
        query_emb,
        query_gain.reshape(1, 128),
        key_gain.reshape(1, 128),
        doc_lengths,
        span_lengths,
        answer_options.T,
    )
    loss, gq, gk, gv = pl.pallas_call(
        hand_over,
        out_shape=(
            jax.ShapeDtypeStruct((QUERIES // NPB,), F32),
            jax.ShapeDtypeStruct((tok, 4096), BF16),
            jax.ShapeDtypeStruct((tok, 1024), BF16),
            jax.ShapeDtypeStruct((tok, 1024), BF16),
        ),
        in_specs=[vmem] * 4,
        out_specs=(vmem, anywhere, anywhere, anywhere),
        scratch_shapes=[dma(3)],
        name="hand_over",
    )(*[pltpu.with_memory_space_constraint(part, pltpu.VMEM) for part in (loss, gq, gk, gv)])
    return loss, gq[None], gk[None], gv[None]


def solution(mesh):
    in_specs = (
        P("pb", "seq", None),
        P("pb", "seq", None),
        P("pb", "seq", None),
        P(),
        P(),
        P("pb", None),
        P("pb", None),
        P("pb", "seq"),
        P(),
    )
    out_specs = (P("pb"), P("pb", "seq", None), P("pb", "seq", None), P("pb", "seq", None))
    return jax.shard_map(
        on_device, mesh=mesh, in_specs=in_specs, out_specs=out_specs, check_vma=False
    )
```

```python
import functools
import math

import jax
import jax.numpy as jnp
from jax import lax
from jax.experimental import pallas as pl
from jax.experimental.pallas import tpu as pltpu
from jax.sharding import PartitionSpec as P

WIDTH = 128
NY = 4
NZ = 8
NPB = 8
BLOCK = 128
ROWS = 512
WINDOW = 1152
CHUNK = 384
SPANS = 128
QUERIES = 512
CAND = 8
EPS = 1e-06
MASKED = 16384.0
LOG2E = math.log2(math.e)
SCALE = 1.0 / math.sqrt(WIDTH)
F32 = jnp.float32
BF16 = jnp.bfloat16
MESH = pl.DeviceIdType.MESH
NT = (((1,), (1,)), ((), ()))


def dot(a, b):
    return jnp.dot(a, b, preferred_element_type=F32)


def dot_nt(a, b):
    return lax.dot_general(a, b, NT, preferred_element_type=F32)


def turned(x):
    return jnp.transpose(x.astype(F32))


def iota(shape, dim):
    return lax.broadcasted_iota(jnp.int32, shape, dim)


def aligned(start, size, unit=128):
    return pl.ds(pl.multiple_of(start, unit), size)


def column(row):
    return jnp.transpose(jnp.broadcast_to(row, (128, 128)))


def segments(lens):
    down = column(lens)
    across = jnp.broadcast_to(lens, (128, 128))
    sub, lane = iota((128, 128), 0), iota((128, 128), 1)
    first_row = jnp.sum(jnp.where(sub < lane, down, 0.0), axis=0, keepdims=True)
    first_col = jnp.sum(jnp.where(lane < sub, across, 0.0), axis=1, keepdims=True)
    return first_row, first_row + lens, first_col, first_col + down[:, :1]


def body(
    q_ref, k_ref, v_ref, e_ref, qgain_ref, kgain_ref, dlen_ref, slen_ref, ans_ref,
    loss_ref, gq_ref, gk_ref, gv_ref,
    qraw, kv, qe, ka, kt, va, vt, qst, qraw_t, qrec, w, ot, ef, sp, sgt, doa, dss, dk, dv,
    dqb, dkb, dvb, hsend, hrecv, hot_c, rsb, zb, pbb, agb, mysc, dli, sli, qgi, kgi, ansi,
    kv_s, kv_r, q_s, q_r, h_s, h_r, e_s, e_r, x_s, x_r, c_s, c_r, loc,
    rs_s, rs_r, z_s, z_r, p_s, p_r, a_s, a_r,
    gq_s, gq_r, bh_s, bh_r, bk_s, bk_r,
):
    me = lax.axis_index("seq")
    pb = lax.axis_index("pb")
    z = me // NY
    y = me % NY
    up = (z + 1) % NZ
    down = (z + NZ - 1) % NZ
    sibling = pb + 1 - 2 * (pb % 2)

    def at(zz, yy):
        return {"seq": zz * NY + yy, "pb": pb}

    def remote(src, dst, ss, rs, dev):
        return pltpu.make_async_remote_copy(
            src_ref=src, dst_ref=dst, send_sem=ss, recv_sem=rs, device_id=dev, device_id_type=MESH
        )

    small = [
        pltpu.make_async_copy(src, dst, loc.at[10 + i])
        for i, (src, dst) in enumerate(
            ((dlen_ref, dli), (slen_ref, sli), (qgain_ref, qgi), (kgain_ref, kgi), (ans_ref, ansi))
        )
    ]
    for copy in small:
        copy.start()

    barrier = pltpu.get_barrier_semaphore()

    def greet(dev):
        pl.semaphore_signal(barrier, inc=1, device_id=dev, device_id_type=MESH)

    for k in range(1, NY):
        greet(at(z, (y + k) % NY))
    for k in range(1, NZ):
        greet(at((z + k) % NZ, y))
    for k in range(1, NPB):
        greet({"seq": me, "pb": (pb + k) % NPB})
    for zi in range(2):
        for k in range(1, NY):

            @pl.when(2 * y + zi != z)
            def _():
                greet(at(2 * y + zi, (y + k) % NY))

    e_yy = z // 2
    e_self = (e_yy == y).astype(jnp.int32)
    pl.semaphore_wait(barrier, NY + NZ + NPB - 3 + jnp.where(e_self == 1, 0, NZ - 1))

    def kv_copy(dy, g, which):
        ty = (y + dy) % NY
        return remote(
            (k_ref if which == 0 else v_ref).at[:, aligned(ty * 256 + g * 128, 128)],
            kv.at[aligned(ROWS + y * BLOCK, BLOCK), pl.ds(g * 256 + which * 128, 128)],
            kv_s.at[dy - 1, g, which],
            kv_r.at[dy - 1, g, which],
            at(z, ty),
        )

    def kv_landed(dy, g, which):
        sy = (y + NY - dy) % NY
        return remote(
            (k_ref if which == 0 else v_ref).at[:, aligned(y * 256 + g * 128, 128)],
            kv.at[aligned(ROWS + sy * BLOCK, BLOCK), pl.ds(g * 256 + which * 128, 128)],
            kv_s.at[dy - 1, g, which],
            kv_r.at[dy - 1, g, which],
            at(z, sy),
        )

    def q_copy(dy, g):
        ty = (y + dy) % NY
        return remote(
            q_ref.at[:, aligned(ty * 1024 + g * 512, 512)],
            qraw.at[aligned(y * BLOCK, BLOCK), aligned(g * 512, 512)],
            q_s.at[dy - 1, g],
            q_r.at[dy - 1, g],
            at(z, ty),
        )

    def q_landed(dy, g):
        sy = (y + NY - dy) % NY
        return remote(
            q_ref.at[:, aligned(y * 1024 + g * 512, 512)],
            qraw.at[aligned(sy * BLOCK, BLOCK), aligned(g * 512, 512)],
            q_s.at[dy - 1, g],
            q_r.at[dy - 1, g],
            at(z, sy),
        )

    own_rows = aligned(ROWS + y * BLOCK, BLOCK)
    local = [
        pltpu.make_async_copy(
            src.at[:, aligned(y * 256 + g * 128, 128)],
            kv.at[own_rows, pl.ds(g * 256 + which * 128, 128)],
            loc.at[15 + 2 * g + which],
        )
        for g in range(2)
        for which, src in enumerate((k_ref, v_ref))
    ] + [
        pltpu.make_async_copy(
            q_ref.at[:, aligned(y * 1024, 1024)], qraw.at[aligned(y * BLOCK, BLOCK), :], loc.at[2]
        ),
        pltpu.make_async_copy(
            e_ref, qe.at[pb, :, aligned((z % 2) * 512 + y * 128, 128)], loc.at[3]
        ),
    ]
    for copy in local[:4]:
        copy.start()
    order = (2, 1, 3)

    def kv_start(g):
        for which in range(2):
            for dy in order:
                kv_copy(dy, g, which).start()

    def q_start(g):
        for dy in order:
            q_copy(dy, g).start()

    kv_start(0)
    local[4].start()

    def halo(b, g, direction):
        cols = pl.ds(g * 256, 256)
        dst_row = b * BLOCK + (0 if direction == 0 else 2 * ROWS)
        return remote(
            kv.at[aligned(ROWS + b * BLOCK, BLOCK), cols],
            kv.at[aligned(dst_row, BLOCK), cols],
            h_s.at[b, g, direction],
            h_r.at[b, g, direction],
            at(up if direction == 0 else down, y),
        )

    for copy in local[:4]:
        copy.wait()
    for direction in range(2):
        halo(y, 0, direction).start()

    def e_copy(k):
        tz = (z + k) % NZ
        col = aligned((z % 2) * 512 + y * 128, 128)
        return remote(e_ref, qe.at[pb, :, col], e_s.at[k], e_r.at[z % 2, y], at(tz, e_yy))

    @pl.when(e_self == 1)
    def _():
        local[5].start()

    for k in range(NZ):
        if k == 0:

            @pl.when(e_self == 0)
            def _():
                e_copy(0).start()
        else:
            e_copy(k).start()

    def forward_halos(g):
        for dy in (1, 3, 2):
            for which in range(2):
                kv_landed(dy, g, which).wait_recv()
            for direction in range(2):
                halo((y + NY - dy) % NY, g, direction).start()

    kv_start(1)
    forward_halos(0)
    q_start(0)

    @pl.when(e_self == 1)
    def _():
        local[5].wait()

    for zi in range(2):
        for yi in range(NY):

            @pl.when(jnp.logical_or(2 * y + zi != z, yi != y))
            def _():
                remote(
                    e_ref, qe.at[pb, :, pl.ds(zi * 512 + yi * 128, 128)], e_s.at[0],
                    e_r.at[zi, yi], at(2 * y + zi, yi),
                ).wait_recv()

    def x_copy(k):
        return remote(
            qe.at[pb], qe.at[pb], x_s.at[k - 1], x_r.at[k - 1],
            {"seq": me, "pb": (pb + 2 * k) % NPB},
        )

    def x_landed(k):
        src = (pb + NPB - 2 * k) % NPB
        return remote(
            qe.at[src], qe.at[src], x_s.at[k - 1], x_r.at[k - 1], {"seq": me, "pb": src}
        )

    def c_copy(k):
        part = (pb + NPB - 2 * k) % NPB
        return remote(
            qe.at[part], qe.at[part], c_s.at[k], c_r.at[k], {"seq": me, "pb": sibling}
        )

    def c_landed(k):
        part = (sibling + NPB - 2 * k) % NPB
        return remote(
            qe.at[part], qe.at[part], c_s.at[k], c_r.at[k], {"seq": me, "pb": sibling}
        )

    for k in (2, 1, 3):
        x_copy(k).start()
    c_copy(0).start()

    for copy in small:
        copy.wait()
    dlen = jnp.concatenate([dli[...].astype(F32), jnp.zeros((1, 112), F32)], axis=1)
    slen = sli[...].astype(F32)
    dfirst_r, dend_r, dfirst_c, dend_c = segments(dlen)
    sfirst_r, send_r, sfirst_c, send_c = segments(slen)
    span_col = column(slen)[:, :1]
    qgain_col = column(qgi[...])[:, :1]
    kgain = kgi[...]
    base = z * ROWS
    tok_c = (base + iota((SPANS, ROWS), 1)).astype(F32)
    hot_c[...] = jnp.where(
        jnp.logical_and(tok_c >= sfirst_c, tok_c < send_c), 1.0, 0.0
    ).astype(BF16)
    tok_k = base - ROWS + iota((3 * ROWS, 128), 0)
    tok_kf = tok_k.astype(F32)
    lane_k = iota((3 * ROWS, 128), 1)
    same = jnp.logical_and(tok_kf >= dfirst_r, tok_kf < dend_r)
    outside = jnp.logical_and(
        lane_k == 127, jnp.logical_or(tok_k < 0, tok_k >= NZ * ROWS)
    )
    kdoc = jnp.where(jnp.logical_or(same, outside), 1.0, 0.0).astype(BF16)
    ones_v = jnp.where(lane_k < 3, 1.0, 0.0).astype(BF16)
    for g in range(2):
        ka[g, :, 128:256] = kdoc
        va[g, :, 128:256] = ones_v
    tok_q = (base + iota((128, ROWS), 1)).astype(F32)
    qdoc = jnp.where(jnp.logical_and(tok_q >= dfirst_c, tok_q < dend_c), 0.0, -MASKED).astype(BF16)
    for r in range(NY):
        tile = jnp.concatenate([qdoc[:, r * BLOCK : (r + 1) * BLOCK]] * 4, axis=1)
        for g in range(2):
            qst[g * NY + r, 128:256, :] = tile
    doa[:, 128:256, :] = jnp.zeros((NY, 128, 512), BF16)
    sp[...] = jnp.zeros_like(sp)

    local[4].wait()
    def prepare(g, block):
        rows = slice(block * ROWS, (block + 1) * ROWS)
        key = kv[rows, g * 256 : g * 256 + 128].astype(F32)
        square = key * key
        high = square.astype(BF16)
        low = (square - high.astype(F32)).astype(BF16)
        mean = dot(jnp.concatenate([high, low], axis=1), jnp.ones((256, 128), BF16)) * (1.0 / WIDTH)
        key = (key * lax.rsqrt(mean + EPS) * kgain).astype(BF16)
        ka[g, rows, 0:128] = key
        kt[g, :, rows] = turned(key).astype(BF16)
        val = kv[rows, g * 256 + 128 : g * 256 + 256]
        va[g, rows, 0:128] = val
        vt[g, :, rows] = turned(val).astype(BF16)

    def forward_group(g):
        prepare(g, 1)
        for b in range(NY):
            for direction in range(2):
                halo(b, g, direction).wait_recv()
        if g == 0:
            for direction in range(2):
                halo(y, 1, direction).start()
            forward_halos(1)
            q_start(1)
        prepare(g, 0)
        prepare(g, 2)

        def tile(i, _):
            r = (y + i) % NY

            @pl.when(i != 0)
            def _():
                q_landed(NY - i, g).wait_recv()

            idx = g * NY + r
            rows = aligned(r * BLOCK, BLOCK)
            x = qraw[rows, aligned(g * 512, 512)]
            x = jnp.concatenate(
                [turned(x[:, h * 128 : (h + 1) * 128]) for h in range(4)], axis=1
            )
            qraw_t[idx] = x.astype(BF16)
            rq = lax.rsqrt(jnp.mean(x * x, axis=0, keepdims=True) + EPS)
            qrec[idx] = rq
            qst[idx, 0:128, :] = (x * rq * qgain_col).astype(BF16)
            rhs = qst[idx]
            total = jnp.zeros((1, 512), F32)
            for c in range(WINDOW // CHUNK):
                part = slice(c * CHUNK, (c + 1) * CHUNK)
                s = dot(ka[g, aligned(r * BLOCK + c * CHUNK, CHUNK), :], rhs)
                e = jnp.exp2(s * (LOG2E * SCALE))
                total = total + jnp.sum(e, axis=0, keepdims=True)
                ef[part, :] = e
            inv = 1.0 / total
            for c in range(WINDOW // CHUNK):
                part = slice(c * CHUNK, (c + 1) * CHUNK)
                w[idx, part, :] = (ef[part, :] * inv).astype(BF16)
            out = dot(vt[g, :, aligned(r * BLOCK, WINDOW)], w[idx]).astype(BF16)
            ot[idx] = out
            table = hot_c[:, rows]
            for h in range(4):
                hc = aligned(g * 512 + h * 128, 128)
                sp[:, hc] += dot_nt(table, out[:, h * 128 : (h + 1) * 128])
            return 0

        lax.fori_loop(0, NY, tile, 0)

    forward_group(0)
    for k in range(1, 4):
        x_landed(k).wait_recv()
        c_copy(k).start()
    forward_group(1)
    for k in range(4):
        c_landed(k).wait_recv()

    emb = qe[...].reshape(QUERIES, 1024)
    span = (sp[...] / span_col).astype(BF16)
    sims = dot_nt(span, emb)
    mine = ansi[...] - pb * SPANS
    span_no = iota((SPANS, QUERIES), 0)
    for j in range(CAND):
        mysc[j : j + 1, :] = jnp.sum(
            jnp.where(span_no == mine[j : j + 1, :], sims, 0.0), axis=0, keepdims=True
        )

    def lanes(t):
        return aligned(t * 128, 128)

    def rs_copy(dy):
        ty = (y + dy) % NY
        return remote(mysc.at[:, lanes(ty)], rsb.at[y], rs_s.at[dy - 1], rs_r.at[dy - 1], at(z, ty))

    def rs_landed(dy):
        sy = (y + NY - dy) % NY
        return remote(mysc.at[:, lanes(y)], rsb.at[sy], rs_s.at[dy - 1], rs_r.at[dy - 1], at(z, sy))

    def z_copy(k):
        return remote(zb.at[z], zb.at[z], z_s.at[k - 1], z_r.at[k - 1], at((z + k) % NZ, y))

    def z_landed(k):
        src = (z + NZ - k) % NZ
        return remote(zb.at[src], zb.at[src], z_s.at[k - 1], z_r.at[k - 1], at(src, y))

    def p_copy(k):
        dev = {"seq": me, "pb": (pb + k) % NPB}
        return remote(pbb.at[pb], pbb.at[pb], p_s.at[k - 1], p_r.at[k - 1], dev)

    def p_landed(k):
        src = (pb + NPB - k) % NPB
        dev = {"seq": me, "pb": src}
        return remote(pbb.at[src], pbb.at[src], p_s.at[k - 1], p_r.at[k - 1], dev)

    def a_copy(dy):
        ty = (y + dy) % NY
        return remote(agb.at[y], agb.at[y], a_s.at[dy - 1], a_r.at[dy - 1], at(z, ty))

    def a_landed(dy):
        sy = (y + NY - dy) % NY
        return remote(agb.at[sy], agb.at[sy], a_s.at[dy - 1], a_r.at[dy - 1], at(z, sy))

    def total_of(buf, count):
        part = buf[0]
        for t in range(1, count):
            part = part + buf[t]
        return part

    far_first = (4, 3, 5, 2, 6, 1, 7)
    for dy in order:
        rs_copy(dy).start()
    rsb[y] = mysc[:, lanes(y)]
    for g in range(2):
        for dy in order:
            q_copy(dy, g).wait_send()
            for which in range(2):
                kv_copy(dy, g, which).wait_send()
    for dy in order:
        rs_landed(dy).wait_recv()
    zb[z] = total_of(rsb, NY)
    for k in far_first:
        z_copy(k).start()
    for g in range(2):
        for direction in range(2):
            for b in range(NY):
                halo(b, g, direction).wait_send()
    for k in far_first:
        z_landed(k).wait_recv()
    pbb[pb] = total_of(zb, NZ)
    for k in far_first:
        p_copy(k).start()
    for k in range(4):
        c_copy(k).wait_send()
    for k in range(1, 4):
        x_copy(k).wait_send()
    for k in range(1, NZ):
        e_copy(k).wait_send()

    @pl.when(e_self == 0)
    def _():
        e_copy(0).wait_send()

    dk[...] = jnp.zeros_like(dk)
    dv[...] = jnp.zeros_like(dv)
    for k in far_first:
        p_landed(k).wait_recv()
    agb[y] = total_of(pbb, NPB)
    for dy in order:
        a_copy(dy).start()
    for dy in order:
        a_landed(dy).wait_recv()
    tiles = [agb[t] for t in range(NY)]
    sims = jnp.concatenate(tiles, axis=1) / 0.05
    ex = jnp.exp(sims)
    den = jnp.sum(ex, axis=0, keepdims=True)
    loss = jnp.log(den) - sims[0:1, :]
    own_loss = jnp.zeros((1, QUERIES // NPB), F32)
    for t in range(NPB):
        size = QUERIES // NPB
        own_loss = jnp.where(pb == t, loss[:, t * size : (t + 1) * size], own_loss)
    loss_ref[...] = own_loss
    hit = (iota((CAND, QUERIES), 0) == 0).astype(F32)
    weight = 256.0 * (ex / den - hit) / 0.05
    dense = jnp.zeros((SPANS, QUERIES), F32)
    for j in range(CAND):
        dense = dense + jnp.where(span_no == mine[j : j + 1, :], weight[j : j + 1, :], 0.0)
    high = dense.astype(BF16)
    low = (dense - high.astype(F32)).astype(BF16)
    sg = ((dot(high, emb) + dot(low, emb)) / span_col).astype(BF16)
    for h in range(8):
        cols = slice(h * 128, (h + 1) * 128)
        sgt[cols, :] = turned(sg[:, cols]).astype(BF16)

    def gq_copy(g, r, slot):
        return remote(
            dqb.at[aligned(r * BLOCK, BLOCK), aligned(g * 512, 512)],
            gq_ref.at[:, aligned(y * 1024 + g * 512, 512)],
            gq_s.at[slot, g],
            gq_r.at[slot, g],
            at(z, r),
        )

    def gq_landed(g, r, slot):
        return remote(
            dqb.at[aligned(r * BLOCK, BLOCK), aligned(g * 512, 512)],
            gq_ref.at[:, aligned(r * 1024 + g * 512, 512)],
            gq_s.at[slot, g],
            gq_r.at[slot, g],
            at(z, r),
        )

    def gq_local(g):
        return pltpu.make_async_copy(
            dqb.at[aligned(y * BLOCK, BLOCK), aligned(g * 512, 512)],
            gq_ref.at[:, aligned(y * 1024 + g * 512, 512)],
            loc.at[4 + g],
        )

    def back_halo(g, which, direction):
        return remote(
            hsend.at[direction, g, which],
            hrecv.at[direction, g, which],
            bh_s.at[direction, g, which],
            bh_r.at[direction, g, which],
            at(down if direction == 0 else up, y),
        )

    def send_halos(g, which, total, factor):
        for direction in range(2):
            first = 2 * ROWS * direction
            hsend[direction, g, which] = (total[g, first : first + ROWS, :] * factor).astype(BF16)
            back_halo(g, which, direction).start()

    def backward_group(g, _):
        def values_tile(r, _):
            idx = g * NY + r
            rows = aligned(r * BLOCK, BLOCK)
            go = dot(sgt[aligned(g * 512, 512), :], hot_c[:, rows])
            go = jnp.concatenate([go[h * 128 : (h + 1) * 128, :] for h in range(4)], axis=1)
            gob = go.astype(BF16)
            delta = jnp.sum(go * ot[idx].astype(F32), axis=0, keepdims=True)
            d0 = delta.astype(BF16).astype(F32)
            d1 = (delta - d0).astype(BF16).astype(F32)
            d2 = delta - d0 - d1
            row = iota((16, 512), 0)
            extra = jnp.where(row == 0, -d0, jnp.where(row == 1, -d1, jnp.where(row == 2, -d2, 0.0)))
            doa[r, 0:128, :] = gob
            doa[r, 128:144, :] = extra.astype(BF16)
            dv[g, aligned(r * BLOCK, WINDOW), :] += dot_nt(w[idx], gob)
            return 0

        lax.fori_loop(0, NY, values_tile, 0)
        send_halos(g, 1, dv, 1.0)

        def tile(i, _):
            off = jnp.where(i == 0, 2, jnp.where(i == 1, 1, jnp.where(i == 2, 3, 0)))
            r = (y + off) % NY
            idx = g * NY + r
            rows = aligned(r * BLOCK, BLOCK)
            rhs = doa[r]
            for c in range(WINDOW // CHUNK):
                dp = dot(va[g, aligned(r * BLOCK + c * CHUNK, CHUNK), :], rhs)
                part = slice(c * CHUNK, (c + 1) * CHUNK)
                dss[part, :] = (w[idx, part, :].astype(F32) * dp).astype(BF16)
            window = aligned(r * BLOCK, WINDOW)
            dk[g, window, :] += dot_nt(dss[...], qst[idx, 0:128, :])
            dq = dot(kt[g, :, window], dss[...])
            x = qraw_t[idx].astype(F32)
            rq = qrec[idx]
            gained = (qgain_col * SCALE) * dq
            mean = jnp.mean(x * gained, axis=0, keepdims=True)
            res = rq * gained - x * (rq * rq * rq * mean)
            for h in range(4):
                dqb[rows, aligned(g * 512 + h * 128, 128)] = turned(
                    res[:, h * 128 : (h + 1) * 128]
                ).astype(BF16)

            @pl.when(i != 3)
            def _():
                gq_copy(g, r, i).start()

            @pl.when(i == 3)
            def _():
                gq_local(g).start()

            return 0

        lax.fori_loop(0, NY, tile, 0)
        send_halos(g, 0, dk, SCALE)
        return 0

    lax.fori_loop(0, 2, backward_group, 0)
    for dy in order:
        rs_copy(dy).wait_send()
        a_copy(dy).wait_send()
    for k in far_first:
        z_copy(k).wait_send()
        p_copy(k).wait_send()

    def bk_copy(dy, g, which):
        ty = (y + dy) % NY
        src, dst = (dkb, gk_ref) if which == 0 else (dvb, gv_ref)
        return remote(
            src.at[aligned(ty * BLOCK, BLOCK), pl.ds(g * 128, 128)],
            dst.at[:, aligned(y * 256 + g * 128, 128)],
            bk_s.at[dy - 1, g, which],
            bk_r.at[dy - 1, g, which],
            at(z, ty),
        )

    def bk_landed(dy, g, which):
        sy = (y + NY - dy) % NY
        src, dst = (dkb, gk_ref) if which == 0 else (dvb, gv_ref)
        return remote(
            src.at[aligned(sy * BLOCK, BLOCK), pl.ds(g * 128, 128)],
            dst.at[:, aligned(sy * 256 + g * 128, 128)],
            bk_s.at[dy - 1, g, which],
            bk_r.at[dy - 1, g, which],
            at(z, sy),
        )

    def bk_local(g, which):
        src, dst = (dkb, gk_ref) if which == 0 else (dvb, gv_ref)
        return pltpu.make_async_copy(
            src.at[aligned(y * BLOCK, BLOCK), pl.ds(g * 128, 128)],
            dst.at[:, aligned(y * 256 + g * 128, 128)],
            loc.at[6 + 2 * g + which],
        )

    for g in range(2):
        cols = slice(g * 128, (g + 1) * 128)
        for direction in range(2):
            back_halo(g, 1, direction).wait_recv()
        vtot = dv[g, ROWS : 2 * ROWS, :] + hrecv[0, g, 1].astype(F32) + hrecv[1, g, 1].astype(F32)
        dvb[:, cols] = vtot.astype(BF16)
        for dy in order:
            bk_copy(dy, g, 1).start()
        bk_local(g, 1).start()
        for direction in range(2):
            back_halo(g, 0, direction).wait_recv()
        ktot = (
            dk[g, ROWS : 2 * ROWS, :] * SCALE
            + hrecv[0, g, 0].astype(F32)
            + hrecv[1, g, 0].astype(F32)
        )
        x = kv[ROWS : 2 * ROWS, g * 256 : g * 256 + 128].astype(F32)
        rec = lax.rsqrt(jnp.mean(x * x, axis=1, keepdims=True) + EPS)
        gained = kgain * ktot
        mean = jnp.mean(x * gained, axis=1, keepdims=True)
        dkb[:, cols] = (rec * gained - x * (rec * rec * rec * mean)).astype(BF16)
        for dy in order:
            bk_copy(dy, g, 0).start()
        bk_local(g, 0).start()

    for g in range(2):
        gq_local(g).wait()
        for slot, off in enumerate((2, 1, 3)):
            gq_copy(g, (y + off) % NY, slot).wait_send()
            gq_landed(g, (y + NY - off) % NY, slot).wait_recv()
        for which in range(2):
            bk_local(g, which).wait()
            for dy in order:
                bk_copy(dy, g, which).wait_send()
                bk_landed(dy, g, which).wait_recv()
            for direction in range(2):
                back_halo(g, which, direction).wait_send()


def hand_over(loss_in, gq_in, gk_in, gv_in, loss, gq, gk, gv, sem):
    copies = [
        pltpu.make_async_copy(src, dst, sem.at[i])
        for i, (src, dst) in enumerate(((gq_in, gq), (gk_in, gk), (gv_in, gv)))
    ]
    for copy in copies:
        copy.start()
    loss[...] = loss_in[0, :]
    for copy in copies:
        copy.wait()


def on_device(
    queries, keys, values, query_gain, key_gain, doc_lengths, span_lengths, query_emb, answer_options
):
    anywhere = pl.BlockSpec(memory_space=pl.ANY)
    vmem = pl.BlockSpec(memory_space=pltpu.VMEM)

    def dma(*shape):
        return pltpu.SemaphoreType.DMA(shape)

    tok = BLOCK
    loss, gq, gk, gv = pl.pallas_call(
        body,
        out_shape=(
            pltpu.VMEM((1, QUERIES // NPB), F32),
            pltpu.VMEM((tok, 4096), BF16),
            pltpu.VMEM((tok, 1024), BF16),
            pltpu.VMEM((tok, 1024), BF16),
        ),
        in_specs=[anywhere] * 9,
        out_specs=(vmem,) * 4,
        scratch_shapes=[
            pltpu.VMEM((ROWS, 1024), BF16),
            pltpu.VMEM((3 * ROWS, 512), BF16),
            pltpu.VMEM((NPB, QUERIES // NPB, 1024), BF16),
            pltpu.VMEM((2, 3 * ROWS, 256), BF16),
            pltpu.VMEM((2, 128, 3 * ROWS), BF16),
            pltpu.VMEM((2, 3 * ROWS, 256), BF16),
            pltpu.VMEM((2, 128, 3 * ROWS), BF16),
            pltpu.VMEM((8, 256, 512), BF16),
            pltpu.VMEM((8, 128, 512), BF16),
            pltpu.VMEM((8, 1, 512), F32),
            pltpu.VMEM((8, WINDOW, 512), BF16),
            pltpu.VMEM((8, 128, 512), BF16),
            pltpu.VMEM((WINDOW, 512), F32),
            pltpu.VMEM((SPANS, 1024), F32),
            pltpu.VMEM((1024, SPANS), BF16),
            pltpu.VMEM((NY, 256, 512), BF16),
            pltpu.VMEM((WINDOW, 512), BF16),
            pltpu.VMEM((2, 3 * ROWS, 128), F32),
            pltpu.VMEM((2, 3 * ROWS, 128), F32),
            pltpu.VMEM((ROWS, 1024), BF16),
            pltpu.VMEM((ROWS, 256), BF16),
            pltpu.VMEM((ROWS, 256), BF16),
            pltpu.VMEM((2, 2, 2, ROWS, 128), BF16),
            pltpu.VMEM((2, 2, 2, ROWS, 128), BF16),
            pltpu.VMEM((SPANS, ROWS), BF16),
            pltpu.VMEM((NY, 8, 128), F32),
            pltpu.VMEM((NZ, 8, 128), F32),
            pltpu.VMEM((NPB, 8, 128), F32),
            pltpu.VMEM((NY, 8, 128), F32),
            pltpu.VMEM((CAND, QUERIES), F32),
            pltpu.VMEM((1, 16), jnp.int32),
            pltpu.VMEM((1, SPANS), jnp.int32),
            pltpu.VMEM((1, 128), F32),
            pltpu.VMEM((1, 128), F32),
            pltpu.VMEM((CAND, QUERIES), jnp.int32),
            dma(3, 2, 2), dma(3, 2, 2),
            dma(3, 2), dma(3, 2),
            dma(NY, 2, 2), dma(NY, 2, 2),
            dma(NZ), dma(2, NY),
            dma(3), dma(3),
            dma(4), dma(4),
            dma(19),
            dma(3), dma(3),
            dma(7), dma(7),
            dma(7), dma(7),
            dma(3), dma(3),
            dma(3, 2), dma(3, 2),
            dma(2, 2, 2), dma(2, 2, 2),
            dma(3, 2, 2), dma(3, 2, 2),
        ],
        compiler_params=pltpu.CompilerParams(
            collective_id=0, has_side_effects=True, vmem_limit_bytes=56 * 1024 * 1024
        ),
        cost_estimate=pl.CostEstimate(
            flops=8 * 6 * 2 * WINDOW * 512 * 128, bytes_accessed=3 << 20, transcendentals=8 * WINDOW * 512
        ),
        name="attention_contrastive",
    )(
        queries[0],
        keys[0],
        values[0],
        query_emb,
        query_gain.reshape(1, 128),
        key_gain.reshape(1, 128),
        doc_lengths,
        span_lengths,
        answer_options.T,
    )
    loss, gq, gk, gv = pl.pallas_call(
        hand_over,
        out_shape=(
            jax.ShapeDtypeStruct((QUERIES // NPB,), F32),
            jax.ShapeDtypeStruct((tok, 4096), BF16),
            jax.ShapeDtypeStruct((tok, 1024), BF16),
            jax.ShapeDtypeStruct((tok, 1024), BF16),
        ),
        in_specs=[vmem] * 4,
        out_specs=(vmem, anywhere, anywhere, anywhere),
        scratch_shapes=[dma(3)],
        name="hand_over",
    )(*[pltpu.with_memory_space_constraint(part, pltpu.VMEM) for part in (loss, gq, gk, gv)])
    return loss, gq[None], gk[None], gv[None]


def solution(mesh):
    in_specs = (
        P("pb", "seq", None),
        P("pb", "seq", None),
        P("pb", "seq", None),
        P(),
        P(),
        P("pb", None),
        P("pb", None),
        P("pb", "seq"),
        P(),
    )
    out_specs = (P("pb"), P("pb", "seq", None), P("pb", "seq", None), P("pb", "seq", None))
    return jax.shard_map(
        on_device, mesh=mesh, in_specs=in_specs, out_specs=out_specs, check_vma=False
    )
```

```python
import functools
import math

import jax
import jax.numpy as jnp
from jax import lax
from jax.experimental import pallas as pl
from jax.experimental.pallas import tpu as pltpu
from jax.sharding import PartitionSpec as P

WIDTH = 128
NY = 4
NZ = 8
NPB = 8
BLOCK = 128
ROWS = 512
WINDOW = 1152
CHUNK = 384
SPANS = 128
QUERIES = 512
CAND = 8
EPS = 1e-06
MASKED = 16384.0
LOG2E = math.log2(math.e)
SCALE = 1.0 / math.sqrt(WIDTH)
F32 = jnp.float32
BF16 = jnp.bfloat16
MESH = pl.DeviceIdType.MESH
NT = (((1,), (1,)), ((), ()))


def dot(a, b):
    return jnp.dot(a, b, preferred_element_type=F32)


def dot_nt(a, b):
    return lax.dot_general(a, b, NT, preferred_element_type=F32)


def turned(x):
    return jnp.transpose(x.astype(F32))


def iota(shape, dim):
    return lax.broadcasted_iota(jnp.int32, shape, dim)


def aligned(start, size, unit=128):
    return pl.ds(pl.multiple_of(start, unit), size)


def column(row):
    return jnp.transpose(jnp.broadcast_to(row, (128, 128)))


def segments(lens):
    down = column(lens)
    across = jnp.broadcast_to(lens, (128, 128))
    sub, lane = iota((128, 128), 0), iota((128, 128), 1)
    first_row = jnp.sum(jnp.where(sub < lane, down, 0.0), axis=0, keepdims=True)
    first_col = jnp.sum(jnp.where(lane < sub, across, 0.0), axis=1, keepdims=True)
    return first_row, first_row + lens, first_col, first_col + down[:, :1]


def body(
    q_ref, k_ref, v_ref, e_ref, qgain_ref, kgain_ref, dlen_ref, slen_ref, ans_ref,
    loss_ref, gq_ref, gk_ref, gv_ref,
    qraw, kv, qe, ka, kt, va, vt, qst, qraw_t, qrec, w, ot, ef, sp, sgt, doa, dss, dk, dv,
    dqb, dkb, dvb, hsend, hrecv, hot_c, rsb, zb, pbb, agb, mysc, dli, sli, qgi, kgi, ansi,
    kv_s, kv_r, q_s, q_r, h_s, h_r, e_s, e_r, x_s, x_r, c_s, c_r, loc,
    rs_s, rs_r, z_s, z_r, p_s, p_r, a_s, a_r,
    gq_s, gq_r, bh_s, bh_r, bk_s, bk_r,
):
    me = lax.axis_index("seq")
    pb = lax.axis_index("pb")
    z = me // NY
    y = me % NY
    up = (z + 1) % NZ
    down = (z + NZ - 1) % NZ
    sibling = pb + 1 - 2 * (pb % 2)

    def at(zz, yy):
        return {"seq": zz * NY + yy, "pb": pb}

    def remote(src, dst, ss, rs, dev):
        return pltpu.make_async_remote_copy(
            src_ref=src, dst_ref=dst, send_sem=ss, recv_sem=rs, device_id=dev, device_id_type=MESH
        )

    small = [
        pltpu.make_async_copy(src, dst, loc.at[10 + i])
        for i, (src, dst) in enumerate(
            ((dlen_ref, dli), (slen_ref, sli), (qgain_ref, qgi), (kgain_ref, kgi), (ans_ref, ansi))
        )
    ]
    for copy in small:
        copy.start()

    barrier = pltpu.get_barrier_semaphore()

    def greet(dev):
        pl.semaphore_signal(barrier, inc=1, device_id=dev, device_id_type=MESH)

    for k in range(1, NY):
        greet(at(z, (y + k) % NY))
    for k in range(1, NZ):
        greet(at((z + k) % NZ, y))
    for k in range(1, NPB):
        greet({"seq": me, "pb": (pb + k) % NPB})
    for zi in range(2):
        for k in range(1, NY):

            @pl.when(2 * y + zi != z)
            def _():
                greet(at(2 * y + zi, (y + k) % NY))

    e_yy = z // 2
    e_self = (e_yy == y).astype(jnp.int32)
    pl.semaphore_wait(barrier, NY + NZ + NPB - 3 + jnp.where(e_self == 1, 0, NZ - 1))

    def kv_copy(dy, g, which):
        ty = (y + dy) % NY
        return remote(
            (k_ref if which == 0 else v_ref).at[:, aligned(ty * 256 + g * 128, 128)],
            kv.at[aligned(ROWS + y * BLOCK, BLOCK), pl.ds(g * 256 + which * 128, 128)],
            kv_s.at[dy - 1, g, which],
            kv_r.at[dy - 1, g, which],
            at(z, ty),
        )

    def kv_landed(dy, g, which):
        sy = (y + NY - dy) % NY
        return remote(
            (k_ref if which == 0 else v_ref).at[:, aligned(y * 256 + g * 128, 128)],
            kv.at[aligned(ROWS + sy * BLOCK, BLOCK), pl.ds(g * 256 + which * 128, 128)],
            kv_s.at[dy - 1, g, which],
            kv_r.at[dy - 1, g, which],
            at(z, sy),
        )

    def q_copy(dy, g):
        ty = (y + dy) % NY
        return remote(
            q_ref.at[:, aligned(ty * 1024 + g * 512, 512)],
            qraw.at[aligned(y * BLOCK, BLOCK), aligned(g * 512, 512)],
            q_s.at[dy - 1, g],
            q_r.at[dy - 1, g],
            at(z, ty),
        )

    def q_landed(dy, g):
        sy = (y + NY - dy) % NY
        return remote(
            q_ref.at[:, aligned(y * 1024 + g * 512, 512)],
            qraw.at[aligned(sy * BLOCK, BLOCK), aligned(g * 512, 512)],
            q_s.at[dy - 1, g],
            q_r.at[dy - 1, g],
            at(z, sy),
        )

    own_rows = aligned(ROWS + y * BLOCK, BLOCK)
    local = [
        pltpu.make_async_copy(
            src.at[:, aligned(y * 256 + g * 128, 128)],
            kv.at[own_rows, pl.ds(g * 256 + which * 128, 128)],
            loc.at[15 + 2 * g + which],
        )
        for g in range(2)
        for which, src in enumerate((k_ref, v_ref))
    ] + [
        pltpu.make_async_copy(
            q_ref.at[:, aligned(y * 1024, 1024)], qraw.at[aligned(y * BLOCK, BLOCK), :], loc.at[2]
        ),
        pltpu.make_async_copy(
            e_ref, qe.at[pb, :, aligned((z % 2) * 512 + y * 128, 128)], loc.at[3]
        ),
    ]
    for copy in local[:4]:
        copy.start()
    order = (2, 1, 3)

    def kv_start(g):
        for which in range(2):
            for dy in order:
                kv_copy(dy, g, which).start()

    def q_start(g):
        for dy in order:
            q_copy(dy, g).start()

    kv_start(0)
    local[4].start()

    def halo(b, g, direction):
        cols = pl.ds(g * 256, 256)
        dst_row = b * BLOCK + (0 if direction == 0 else 2 * ROWS)
        return remote(
            kv.at[aligned(ROWS + b * BLOCK, BLOCK), cols],
            kv.at[aligned(dst_row, BLOCK), cols],
            h_s.at[b, g, direction],
            h_r.at[b, g, direction],
            at(up if direction == 0 else down, y),
        )

    for copy in local[:4]:
        copy.wait()
    for direction in range(2):
        halo(y, 0, direction).start()

    def e_copy(k):
        tz = (z + k) % NZ
        col = aligned((z % 2) * 512 + y * 128, 128)
        return remote(e_ref, qe.at[pb, :, col], e_s.at[k], e_r.at[z % 2, y], at(tz, e_yy))

    @pl.when(e_self == 1)
    def _():
        local[5].start()

    for k in range(NZ):
        if k == 0:

            @pl.when(e_self == 0)
            def _():
                e_copy(0).start()
        else:
            e_copy(k).start()

    def forward_halos(g):
        for dy in (1, 3, 2):
            for which in range(2):
                kv_landed(dy, g, which).wait_recv()
            for direction in range(2):
                halo((y + NY - dy) % NY, g, direction).start()

    kv_start(1)
    forward_halos(0)
    q_start(0)

    @pl.when(e_self == 1)
    def _():
        local[5].wait()

    for zi in range(2):
        for yi in range(NY):

            @pl.when(jnp.logical_or(2 * y + zi != z, yi != y))
            def _():
                remote(
                    e_ref, qe.at[pb, :, pl.ds(zi * 512 + yi * 128, 128)], e_s.at[0],
                    e_r.at[zi, yi], at(2 * y + zi, yi),
                ).wait_recv()

    def x_copy(k):
        return remote(
            qe.at[pb], qe.at[pb], x_s.at[k - 1], x_r.at[k - 1],
            {"seq": me, "pb": (pb + 2 * k) % NPB},
        )

    def x_landed(k):
        src = (pb + NPB - 2 * k) % NPB
        return remote(
            qe.at[src], qe.at[src], x_s.at[k - 1], x_r.at[k - 1], {"seq": me, "pb": src}
        )

    def c_copy(k):
        part = (pb + NPB - 2 * k) % NPB
        return remote(
            qe.at[part], qe.at[part], c_s.at[k], c_r.at[k], {"seq": me, "pb": sibling}
        )

    def c_landed(k):
        part = (sibling + NPB - 2 * k) % NPB
        return remote(
            qe.at[part], qe.at[part], c_s.at[k], c_r.at[k], {"seq": me, "pb": sibling}
        )

    for k in (2, 1, 3):
        x_copy(k).start()
    c_copy(0).start()

    for copy in small:
        copy.wait()
    dlen = jnp.concatenate([dli[...].astype(F32), jnp.zeros((1, 112), F32)], axis=1)
    slen = sli[...].astype(F32)
    dfirst_r, dend_r, dfirst_c, dend_c = segments(dlen)
    sfirst_r, send_r, sfirst_c, send_c = segments(slen)
    span_col = column(slen)[:, :1]
    qgain_col = column(qgi[...])[:, :1]
    kgain = kgi[...]
    base = z * ROWS
    tok_c = (base + iota((SPANS, ROWS), 1)).astype(F32)
    hot_c[...] = jnp.where(
        jnp.logical_and(tok_c >= sfirst_c, tok_c < send_c), 1.0, 0.0
    ).astype(BF16)
    tok_k = base - ROWS + iota((3 * ROWS, 128), 0)
    tok_kf = tok_k.astype(F32)
    lane_k = iota((3 * ROWS, 128), 1)
    same = jnp.logical_and(tok_kf >= dfirst_r, tok_kf < dend_r)
    outside = jnp.logical_and(
        lane_k == 127, jnp.logical_or(tok_k < 0, tok_k >= NZ * ROWS)
    )
    kdoc = jnp.where(jnp.logical_or(same, outside), 1.0, 0.0).astype(BF16)
    ones_v = jnp.where(lane_k < 3, 1.0, 0.0).astype(BF16)
    for g in range(2):
        ka[g, :, 128:256] = kdoc
        va[g, :, 128:256] = ones_v
    tok_q = (base + iota((128, ROWS), 1)).astype(F32)
    qdoc = jnp.where(jnp.logical_and(tok_q >= dfirst_c, tok_q < dend_c), 0.0, -MASKED).astype(BF16)
    for r in range(NY):
        tile = jnp.concatenate([qdoc[:, r * BLOCK : (r + 1) * BLOCK]] * 4, axis=1)
        for g in range(2):
            qst[g * NY + r, 128:256, :] = tile
    doa[:, 128:256, :] = jnp.zeros((NY, 128, 512), BF16)
    sp[...] = jnp.zeros_like(sp)

    local[4].wait()
    def prepare(g, block):
        rows = slice(block * ROWS, (block + 1) * ROWS)
        key = kv[rows, g * 256 : g * 256 + 128].astype(F32)
        square = key * key
        high = square.astype(BF16)
        low = (square - high.astype(F32)).astype(BF16)
        mean = dot(jnp.concatenate([high, low], axis=1), jnp.ones((256, 128), BF16)) * (1.0 / WIDTH)
        key = (key * lax.rsqrt(mean + EPS) * kgain).astype(BF16)
        ka[g, rows, 0:128] = key
        kt[g, :, rows] = turned(key).astype(BF16)
        val = kv[rows, g * 256 + 128 : g * 256 + 256]
        va[g, rows, 0:128] = val
        vt[g, :, rows] = turned(val).astype(BF16)

    def forward_group(g):
        prepare(g, 1)
        for b in range(NY):
            for direction in range(2):
                halo(b, g, direction).wait_recv()
        if g == 0:
            for direction in range(2):
                halo(y, 1, direction).start()
            forward_halos(1)
            q_start(1)
        prepare(g, 0)
        prepare(g, 2)

        def tile(i, _):
            off = jnp.where(i == 2, 3, jnp.where(i == 3, 2, i))
            r = (y + off) % NY

            @pl.when(i != 0)
            def _():
                q_landed(NY - off, g).wait_recv()

            idx = g * NY + r
            rows = aligned(r * BLOCK, BLOCK)
            x = qraw[rows, aligned(g * 512, 512)]
            x = jnp.concatenate(
                [turned(x[:, h * 128 : (h + 1) * 128]) for h in range(4)], axis=1
            )
            qraw_t[idx] = x.astype(BF16)
            rq = lax.rsqrt(jnp.mean(x * x, axis=0, keepdims=True) + EPS)
            qrec[idx] = rq
            qst[idx, 0:128, :] = (x * rq * qgain_col).astype(BF16)
            rhs = qst[idx]
            total = jnp.zeros((1, 512), F32)
            for c in range(WINDOW // CHUNK):
                part = slice(c * CHUNK, (c + 1) * CHUNK)
                s = dot(ka[g, aligned(r * BLOCK + c * CHUNK, CHUNK), :], rhs)
                e = jnp.exp2(s * (LOG2E * SCALE))
                total = total + jnp.sum(e, axis=0, keepdims=True)
                ef[part, :] = e
            inv = 1.0 / total
            for c in range(WINDOW // CHUNK):
                part = slice(c * CHUNK, (c + 1) * CHUNK)
                w[idx, part, :] = (ef[part, :] * inv).astype(BF16)
            out = dot(vt[g, :, aligned(r * BLOCK, WINDOW)], w[idx]).astype(BF16)
            ot[idx] = out
            table = hot_c[:, rows]
            for h in range(4):
                hc = aligned(g * 512 + h * 128, 128)
                sp[:, hc] += dot_nt(table, out[:, h * 128 : (h + 1) * 128])
            return 0

        lax.fori_loop(0, NY, tile, 0)

    forward_group(0)
    for k in range(1, 4):
        x_landed(k).wait_recv()
        c_copy(k).start()
    forward_group(1)
    for k in range(4):
        c_landed(k).wait_recv()

    emb = qe[...].reshape(QUERIES, 1024)
    span = (sp[...] / span_col).astype(BF16)
    sims = dot_nt(span, emb)
    mine = ansi[...] - pb * SPANS
    span_no = iota((SPANS, QUERIES), 0)
    for j in range(CAND):
        mysc[j : j + 1, :] = jnp.sum(
            jnp.where(span_no == mine[j : j + 1, :], sims, 0.0), axis=0, keepdims=True
        )

    def lanes(t):
        return aligned(t * 128, 128)

    def rs_copy(dy):
        ty = (y + dy) % NY
        return remote(mysc.at[:, lanes(ty)], rsb.at[y], rs_s.at[dy - 1], rs_r.at[dy - 1], at(z, ty))

    def rs_landed(dy):
        sy = (y + NY - dy) % NY
        return remote(mysc.at[:, lanes(y)], rsb.at[sy], rs_s.at[dy - 1], rs_r.at[dy - 1], at(z, sy))

    def z_copy(k):
        return remote(zb.at[z], zb.at[z], z_s.at[k - 1], z_r.at[k - 1], at((z + k) % NZ, y))

    def z_landed(k):
        src = (z + NZ - k) % NZ
        return remote(zb.at[src], zb.at[src], z_s.at[k - 1], z_r.at[k - 1], at(src, y))

    def p_copy(k):
        dev = {"seq": me, "pb": (pb + k) % NPB}
        return remote(pbb.at[pb], pbb.at[pb], p_s.at[k - 1], p_r.at[k - 1], dev)

    def p_landed(k):
        src = (pb + NPB - k) % NPB
        dev = {"seq": me, "pb": src}
        return remote(pbb.at[src], pbb.at[src], p_s.at[k - 1], p_r.at[k - 1], dev)

    def a_copy(dy):
        ty = (y + dy) % NY
        return remote(agb.at[y], agb.at[y], a_s.at[dy - 1], a_r.at[dy - 1], at(z, ty))

    def a_landed(dy):
        sy = (y + NY - dy) % NY
        return remote(agb.at[sy], agb.at[sy], a_s.at[dy - 1], a_r.at[dy - 1], at(z, sy))

    def total_of(buf, count):
        part = buf[0]
        for t in range(1, count):
            part = part + buf[t]
        return part

    far_first = (4, 3, 5, 2, 6, 1, 7)
    for dy in order:
        rs_copy(dy).start()
    rsb[y] = mysc[:, lanes(y)]
    for g in range(2):
        for dy in order:
            q_copy(dy, g).wait_send()
            for which in range(2):
                kv_copy(dy, g, which).wait_send()
    for dy in order:
        rs_landed(dy).wait_recv()
    zb[z] = total_of(rsb, NY)
    for k in far_first:
        z_copy(k).start()
    for g in range(2):
        for direction in range(2):
            for b in range(NY):
                halo(b, g, direction).wait_send()
    for k in far_first:
        z_landed(k).wait_recv()
    pbb[pb] = total_of(zb, NZ)
    for k in far_first:
        p_copy(k).start()
    for k in range(4):
        c_copy(k).wait_send()
    for k in range(1, 4):
        x_copy(k).wait_send()
    for k in range(1, NZ):
        e_copy(k).wait_send()

    @pl.when(e_self == 0)
    def _():
        e_copy(0).wait_send()

    dk[...] = jnp.zeros_like(dk)
    dv[...] = jnp.zeros_like(dv)
    for k in far_first:
        p_landed(k).wait_recv()
    agb[y] = total_of(pbb, NPB)
    for dy in order:
        a_copy(dy).start()
    for dy in order:
        a_landed(dy).wait_recv()
    tiles = [agb[t] for t in range(NY)]
    sims = jnp.concatenate(tiles, axis=1) / 0.05
    ex = jnp.exp(sims)
    den = jnp.sum(ex, axis=0, keepdims=True)
    loss = jnp.log(den) - sims[0:1, :]
    own_loss = jnp.zeros((1, QUERIES // NPB), F32)
    for t in range(NPB):
        size = QUERIES // NPB
        own_loss = jnp.where(pb == t, loss[:, t * size : (t + 1) * size], own_loss)
    loss_ref[...] = own_loss
    hit = (iota((CAND, QUERIES), 0) == 0).astype(F32)
    weight = 256.0 * (ex / den - hit) / 0.05
    dense = jnp.zeros((SPANS, QUERIES), F32)
    for j in range(CAND):
        dense = dense + jnp.where(span_no == mine[j : j + 1, :], weight[j : j + 1, :], 0.0)
    high = dense.astype(BF16)
    low = (dense - high.astype(F32)).astype(BF16)
    sg = ((dot(high, emb) + dot(low, emb)) / span_col).astype(BF16)
    for h in range(8):
        cols = slice(h * 128, (h + 1) * 128)
        sgt[cols, :] = turned(sg[:, cols]).astype(BF16)

    def gq_copy(g, r, slot):
        return remote(
            dqb.at[aligned(r * BLOCK, BLOCK), aligned(g * 512, 512)],
            gq_ref.at[:, aligned(y * 1024 + g * 512, 512)],
            gq_s.at[slot, g],
            gq_r.at[slot, g],
            at(z, r),
        )

    def gq_landed(g, r, slot):
        return remote(
            dqb.at[aligned(r * BLOCK, BLOCK), aligned(g * 512, 512)],
            gq_ref.at[:, aligned(r * 1024 + g * 512, 512)],
            gq_s.at[slot, g],
            gq_r.at[slot, g],
            at(z, r),
        )

    def gq_local(g):
        return pltpu.make_async_copy(
            dqb.at[aligned(y * BLOCK, BLOCK), aligned(g * 512, 512)],
            gq_ref.at[:, aligned(y * 1024 + g * 512, 512)],
            loc.at[4 + g],
        )

    def back_halo(g, which, direction):
        return remote(
            hsend.at[direction, g, which],
            hrecv.at[direction, g, which],
            bh_s.at[direction, g, which],
            bh_r.at[direction, g, which],
            at(down if direction == 0 else up, y),
        )

    def send_halos(g, which, total, factor):
        for direction in range(2):
            first = 2 * ROWS * direction
            hsend[direction, g, which] = (total[g, first : first + ROWS, :] * factor).astype(BF16)
            back_halo(g, which, direction).start()

    def backward_group(g, _):
        def values_tile(r, _):
            idx = g * NY + r
            rows = aligned(r * BLOCK, BLOCK)
            go = dot(sgt[aligned(g * 512, 512), :], hot_c[:, rows])
            go = jnp.concatenate([go[h * 128 : (h + 1) * 128, :] for h in range(4)], axis=1)
            gob = go.astype(BF16)
            delta = jnp.sum(go * ot[idx].astype(F32), axis=0, keepdims=True)
            d0 = delta.astype(BF16).astype(F32)
            d1 = (delta - d0).astype(BF16).astype(F32)
            d2 = delta - d0 - d1
            row = iota((16, 512), 0)
            extra = jnp.where(row == 0, -d0, jnp.where(row == 1, -d1, jnp.where(row == 2, -d2, 0.0)))
            doa[r, 0:128, :] = gob
            doa[r, 128:144, :] = extra.astype(BF16)
            dv[g, aligned(r * BLOCK, WINDOW), :] += dot_nt(w[idx], gob)
            return 0

        lax.fori_loop(0, NY, values_tile, 0)
        send_halos(g, 1, dv, 1.0)

        def tile(i, _):
            off = jnp.where(i == 0, 2, jnp.where(i == 1, 1, jnp.where(i == 2, 3, 0)))
            r = (y + off) % NY
            idx = g * NY + r
            rows = aligned(r * BLOCK, BLOCK)
            rhs = doa[r]
            for c in range(WINDOW // CHUNK):
                dp = dot(va[g, aligned(r * BLOCK + c * CHUNK, CHUNK), :], rhs)
                part = slice(c * CHUNK, (c + 1) * CHUNK)
                dss[part, :] = (w[idx, part, :].astype(F32) * dp).astype(BF16)
            window = aligned(r * BLOCK, WINDOW)
            dk[g, window, :] += dot_nt(dss[...], qst[idx, 0:128, :])
            dq = dot(kt[g, :, window], dss[...])
            x = qraw_t[idx].astype(F32)
            rq = qrec[idx]
            gained = (qgain_col * SCALE) * dq
            mean = jnp.mean(x * gained, axis=0, keepdims=True)
            res = rq * gained - x * (rq * rq * rq * mean)
            for h in range(4):
                dqb[rows, aligned(g * 512 + h * 128, 128)] = turned(
                    res[:, h * 128 : (h + 1) * 128]
                ).astype(BF16)

            @pl.when(i != 3)
            def _():
                gq_copy(g, r, i).start()

            @pl.when(i == 3)
            def _():
                gq_local(g).start()

            return 0

        lax.fori_loop(0, NY, tile, 0)
        send_halos(g, 0, dk, SCALE)
        return 0

    lax.fori_loop(0, 2, backward_group, 0)

    def bk_copy(dy, g, which):
        ty = (y + dy) % NY
        src, dst = (dkb, gk_ref) if which == 0 else (dvb, gv_ref)
        return remote(
            src.at[aligned(ty * BLOCK, BLOCK), pl.ds(g * 128, 128)],
            dst.at[:, aligned(y * 256 + g * 128, 128)],
            bk_s.at[dy - 1, g, which],
            bk_r.at[dy - 1, g, which],
            at(z, ty),
        )

    def bk_landed(dy, g, which):
        sy = (y + NY - dy) % NY
        src, dst = (dkb, gk_ref) if which == 0 else (dvb, gv_ref)
        return remote(
            src.at[aligned(sy * BLOCK, BLOCK), pl.ds(g * 128, 128)],
            dst.at[:, aligned(sy * 256 + g * 128, 128)],
            bk_s.at[dy - 1, g, which],
            bk_r.at[dy - 1, g, which],
            at(z, sy),
        )

    def bk_local(g, which):
        src, dst = (dkb, gk_ref) if which == 0 else (dvb, gv_ref)
        return pltpu.make_async_copy(
            src.at[aligned(y * BLOCK, BLOCK), pl.ds(g * 128, 128)],
            dst.at[:, aligned(y * 256 + g * 128, 128)],
            loc.at[6 + 2 * g + which],
        )

    for g in range(2):
        if g == 1:
            for dy in order:
                rs_copy(dy).wait_send()
                a_copy(dy).wait_send()
            for k in far_first:
                z_copy(k).wait_send()
                p_copy(k).wait_send()
        cols = slice(g * 128, (g + 1) * 128)
        for direction in range(2):
            back_halo(g, 1, direction).wait_recv()
        vtot = dv[g, ROWS : 2 * ROWS, :] + hrecv[0, g, 1].astype(F32) + hrecv[1, g, 1].astype(F32)
        dvb[:, cols] = vtot.astype(BF16)
        for dy in order:
            bk_copy(dy, g, 1).start()
        bk_local(g, 1).start()
        for direction in range(2):
            back_halo(g, 0, direction).wait_recv()
        ktot = (
            dk[g, ROWS : 2 * ROWS, :] * SCALE
            + hrecv[0, g, 0].astype(F32)
            + hrecv[1, g, 0].astype(F32)
        )
        x = kv[ROWS : 2 * ROWS, g * 256 : g * 256 + 128].astype(F32)
        rec = lax.rsqrt(jnp.mean(x * x, axis=1, keepdims=True) + EPS)
        gained = kgain * ktot
        mean = jnp.mean(x * gained, axis=1, keepdims=True)
        dkb[:, cols] = (rec * gained - x * (rec * rec * rec * mean)).astype(BF16)
        for dy in order:
            bk_copy(dy, g, 0).start()
        bk_local(g, 0).start()

    for g in range(2):
        gq_local(g).wait()
        for slot, off in enumerate((2, 1, 3)):
            gq_copy(g, (y + off) % NY, slot).wait_send()
            gq_landed(g, (y + NY - off) % NY, slot).wait_recv()
        for which in range(2):
            bk_local(g, which).wait()
            for dy in order:
                bk_copy(dy, g, which).wait_send()
                bk_landed(dy, g, which).wait_recv()
            for direction in range(2):
                back_halo(g, which, direction).wait_send()


def hand_over(loss_in, gq_in, gk_in, gv_in, loss, gq, gk, gv, sem):
    copies = [
        pltpu.make_async_copy(src, dst, sem.at[i])
        for i, (src, dst) in enumerate(((gq_in, gq), (gk_in, gk), (gv_in, gv)))
    ]
    for copy in copies:
        copy.start()
    loss[...] = loss_in[0, :]
    for copy in copies:
        copy.wait()


def on_device(
    queries, keys, values, query_gain, key_gain, doc_lengths, span_lengths, query_emb, answer_options
):
    anywhere = pl.BlockSpec(memory_space=pl.ANY)
    vmem = pl.BlockSpec(memory_space=pltpu.VMEM)

    def dma(*shape):
        return pltpu.SemaphoreType.DMA(shape)

    tok = BLOCK
    loss, gq, gk, gv = pl.pallas_call(
        body,
        out_shape=(
            pltpu.VMEM((1, QUERIES // NPB), F32),
            pltpu.VMEM((tok, 4096), BF16),
            pltpu.VMEM((tok, 1024), BF16),
            pltpu.VMEM((tok, 1024), BF16),
        ),
        in_specs=[anywhere] * 9,
        out_specs=(vmem,) * 4,
        scratch_shapes=[
            pltpu.VMEM((ROWS, 1024), BF16),
            pltpu.VMEM((3 * ROWS, 512), BF16),
            pltpu.VMEM((NPB, QUERIES // NPB, 1024), BF16),
            pltpu.VMEM((2, 3 * ROWS, 256), BF16),
            pltpu.VMEM((2, 128, 3 * ROWS), BF16),
            pltpu.VMEM((2, 3 * ROWS, 256), BF16),
            pltpu.VMEM((2, 128, 3 * ROWS), BF16),
            pltpu.VMEM((8, 256, 512), BF16),
            pltpu.VMEM((8, 128, 512), BF16),
            pltpu.VMEM((8, 1, 512), F32),
            pltpu.VMEM((8, WINDOW, 512), BF16),
            pltpu.VMEM((8, 128, 512), BF16),
            pltpu.VMEM((WINDOW, 512), F32),
            pltpu.VMEM((SPANS, 1024), F32),
            pltpu.VMEM((1024, SPANS), BF16),
            pltpu.VMEM((NY, 256, 512), BF16),
            pltpu.VMEM((WINDOW, 512), BF16),
            pltpu.VMEM((2, 3 * ROWS, 128), F32),
            pltpu.VMEM((2, 3 * ROWS, 128), F32),
            pltpu.VMEM((ROWS, 1024), BF16),
            pltpu.VMEM((ROWS, 256), BF16),
            pltpu.VMEM((ROWS, 256), BF16),
            pltpu.VMEM((2, 2, 2, ROWS, 128), BF16),
            pltpu.VMEM((2, 2, 2, ROWS, 128), BF16),
            pltpu.VMEM((SPANS, ROWS), BF16),
            pltpu.VMEM((NY, 8, 128), F32),
            pltpu.VMEM((NZ, 8, 128), F32),
            pltpu.VMEM((NPB, 8, 128), F32),
            pltpu.VMEM((NY, 8, 128), F32),
            pltpu.VMEM((CAND, QUERIES), F32),
            pltpu.VMEM((1, 16), jnp.int32),
            pltpu.VMEM((1, SPANS), jnp.int32),
            pltpu.VMEM((1, 128), F32),
            pltpu.VMEM((1, 128), F32),
            pltpu.VMEM((CAND, QUERIES), jnp.int32),
            dma(3, 2, 2), dma(3, 2, 2),
            dma(3, 2), dma(3, 2),
            dma(NY, 2, 2), dma(NY, 2, 2),
            dma(NZ), dma(2, NY),
            dma(3), dma(3),
            dma(4), dma(4),
            dma(19),
            dma(3), dma(3),
            dma(7), dma(7),
            dma(7), dma(7),
            dma(3), dma(3),
            dma(3, 2), dma(3, 2),
            dma(2, 2, 2), dma(2, 2, 2),
            dma(3, 2, 2), dma(3, 2, 2),
        ],
        compiler_params=pltpu.CompilerParams(
            collective_id=0, has_side_effects=True, vmem_limit_bytes=56 * 1024 * 1024
        ),
        cost_estimate=pl.CostEstimate(
            flops=8 * 6 * 2 * WINDOW * 512 * 128, bytes_accessed=3 << 20, transcendentals=8 * WINDOW * 512
        ),
        name="attention_contrastive",
    )(
        queries[0],
        keys[0],
        values[0],
        query_emb,
        query_gain.reshape(1, 128),
        key_gain.reshape(1, 128),
        doc_lengths,
        span_lengths,
        answer_options.T,
    )
    loss, gq, gk, gv = pl.pallas_call(
        hand_over,
        out_shape=(
            jax.ShapeDtypeStruct((QUERIES // NPB,), F32),
            jax.ShapeDtypeStruct((tok, 4096), BF16),
            jax.ShapeDtypeStruct((tok, 1024), BF16),
            jax.ShapeDtypeStruct((tok, 1024), BF16),
        ),
        in_specs=[vmem] * 4,
        out_specs=(vmem, anywhere, anywhere, anywhere),
        scratch_shapes=[dma(3)],
        name="hand_over",
    )(*[pltpu.with_memory_space_constraint(part, pltpu.VMEM) for part in (loss, gq, gk, gv)])
    return loss, gq[None], gk[None], gv[None]


def solution(mesh):
    in_specs = (
        P("pb", "seq", None),
        P("pb", "seq", None),
        P("pb", "seq", None),
        P(),
        P(),
        P("pb", None),
        P("pb", None),
        P("pb", "seq"),
        P(),
    )
    out_specs = (P("pb"), P("pb", "seq", None), P("pb", "seq", None), P("pb", "seq", None))
    return jax.shard_map(
        on_device, mesh=mesh, in_specs=in_specs, out_specs=out_specs, check_vma=False
    )
```
